256 devices in a mesh: lat: 4 (over x_lo, core), lon: 64 (over z, x_hi, y).
Axes of the slice: x: 4 (x_hi: 2, x_lo: 2; x = x_hi * 2 + x_lo), y: 4, z: 8, core: 2. Of those that a mesh axis runs over, the one named last changes fastest.
Arguments:
- pre_act: bfloat16 [8, 49152, 512], P('lat', 'lon'), may hold values from -18 to 18
- grad_out: bfloat16 [8, 49152, 512], P('lat', 'lon'), may hold values from -61 to 61
- kernel: bfloat16 [3, 3, 512, 512], replicated, may hold values from -0.09375 to 0.09375
Outputs:
- grad_in: bfloat16 [8, 49152, 512], P('lat', 'lon')
- grad_kernel: float32 [512, 3, 3, 512], P('lon', None, None, 'lat')
The draws below stay inside these ranges and needn't reach their ends.
All inputs are finite; a program needn't handle non-finite values.
Results may differ from the reference program's by a relative error of at most 0.0028.
Values may be sent and summed in bfloat16 or wider, within the bound.
A program may use at most 128 MiB of HBM per device.

```python
import jax
import jax.numpy as jnp
from jax import lax

C = 512
ROWS = 8
LON = 49152


def draw_grad_out(key, part):
    key = jax.random.fold_in(key, 21)
    key_noise = jax.random.fold_in(key, 1)
    key_channel = jax.random.fold_in(key, 3)
    key_cells = jax.random.fold_in(key, 4)
    noise_base = jax.random.truncated_normal(key_noise, -4.0, 4.0, (ROWS, LON, C), jnp.float32)
    lift_rate = 0.8
    channel_scale = jnp.exp(jax.random.uniform(key_channel, (1, 1, C), jnp.float32, jnp.log(0.3), jnp.log(3.0)))
    cell_rough = jnp.exp(jax.random.uniform(key_cells, (ROWS, LON, 1), jnp.float32, jnp.log(0.7), jnp.log(1.4)))
    lon_rise = 1.0 + jnp.arange(LON, dtype=jnp.float32)[None, :, None] / LON
    channel_rise = 1.0 + lift_rate * jnp.arange(C, dtype=jnp.float32)[None, None, :] / C
    return (noise_base * channel_scale * cell_rough * lon_rise * channel_rise).astype(jnp.bfloat16)


def draw_pre_act(key, part):
    key = jax.random.fold_in(key, 31)
    key_noise = jax.random.fold_in(key, 1)
    key_channel = jax.random.fold_in(key, 2)
    noise_base = jax.random.truncated_normal(key_noise, -4.0, 4.0, (ROWS, LON, C), jnp.float32)
    channel_scale = jnp.exp(jax.random.uniform(key_channel, (1, 1, C), jnp.float32, jnp.log(0.3), jnp.log(3.0)))
    channel_rise = 1.0 + 0.5 * jnp.arange(C, dtype=jnp.float32)[None, None, :] / C
    return (noise_base * channel_scale * channel_rise).astype(jnp.bfloat16)


def bell_draw(stream_key, dims, spread, most, kind=jnp.bfloat16):
    result = jax.random.normal(stream_key, dims, jnp.float32) * spread
    return jnp.minimum(jnp.maximum(result, -most), most).astype(kind)


def setup_inputs(seed: int = 0) -> dict:
    splits = jax.random.split(jax.random.key(seed), 4)
    return {
        "pre_act": draw_pre_act(jax.random.fold_in(splits[3], 71), 0),
        "grad_out": draw_grad_out(jax.random.fold_in(splits[3], 71), 0),
        "kernel": bell_draw(splits[2], (3, 3, C, C), (9 * C) ** -0.5, 0.09375),
    }


def extend(field):
    padded = jnp.pad(field, ((1, 1), (0, 0), (0, 0)))
    return jnp.concatenate([padded[:, -1:], padded, padded[:, :1]], axis=1)

def reference(pre_act, grad_out, kernel):
    breadth = pre_act.shape[1]
    padded = extend(grad_out)

    def one_row(running, row_index):
        window = lax.dynamic_slice_in_dim(padded, row_index, 3, 0)
        pre_wide = lax.dynamic_index_in_dim(pre_act, row_index, 0, keepdims=False).astype(jnp.float32)
        activated = jax.nn.silu(pre_wide).astype(jnp.bfloat16)
        grad_act = jnp.zeros((breadth, C), jnp.float32)
        blocks = []
        for lat_off in (-1, 0, 1):
            for lon_off in (-1, 0, 1):
                shifted = window[1 - lat_off, 1 - lon_off:1 - lon_off + breadth]
                grad_act = grad_act + jnp.dot(shifted, kernel[lat_off + 1, lon_off + 1].T, preferred_element_type=jnp.float32)
                blocks.append(jnp.dot(shifted.T, activated, preferred_element_type=jnp.float32))
        sigmoid_pre = jax.nn.sigmoid(pre_wide)
        grad_row = (grad_act * sigmoid_pre * (1.0 + pre_wide * (1.0 - sigmoid_pre))).astype(jnp.bfloat16)
        return (running + jnp.stack(blocks, axis=1).reshape(C, 3, 3, C), grad_row)
    start_sum = jnp.zeros((C, 3, 3, C), jnp.float32)
    summed, grad_in = lax.scan(one_row, start_sum, jnp.arange(ROWS, dtype=jnp.int32))
    grand_total = jnp.sum(summed * summed)
    factor = jnp.float32(3.0 * C) / jnp.sqrt(grand_total + 1e-06)
    return (grad_in, factor * summed)
```

```python
import jax
import jax.numpy as jnp
from jax import lax
from jax.experimental import pallas as pl
from jax.experimental.pallas import tpu as pltpu
from jax.sharding import PartitionSpec as P

BF = jnp.bfloat16
F32 = jnp.float32
MESH = pl.DeviceIdType.MESH
B = 768
C = 512
TN = (((0,), (0,)), ((), ()))
NT = (((1,), (1,)), ((), ()))


def sigmoid(v):
    return 1.0 / (1.0 + jnp.exp(-v))


def body(
    pre_hbm, go_hbm, w_hbm, gin_hbm, gk_ref,
    ext, gos, wv, pre_half, pre_own, act, acc, gin,
    px, send_x, recv_x, zx, send_zx, recv_zx, send_yf, recv_yf,
    py, send_y, recv_y, zy, send_z, recv_z, send_xf, recv_xf,
    final, ar_own, ar_core, ar_y, ar_x, ar_z,
    ld_sem, w_sem, out_sem, sib_s, sib_r, rim_s, rim_r, halo_s, halo_r, hrim_s, hrim_r, fwd_s, fwd_r,
    x_s, x_r, zx_s, zx_r, yf_s, yf_r, y_s, y_r, z_s, z_r, xf_s, xf_r, ar_s, ar_r,
):
    lat = lax.axis_index("lat")
    lon = lax.axis_index("lon")
    xlo, core = lat // 2, lat % 2
    z, xh, y = lon // 8, (lon // 4) % 2, lon % 4
    x = xh * 2 + xlo

    sib = (xlo * 2 + 1 - core, lon)
    left, right = lax.rem(lon + 63, 64), lax.rem(lon + 1, 64)

    def y_peer(d):
        to = lax.rem(y + d, 4)
        return to, (lat, (z * 2 + xh) * 4 + to)

    def z_peer(d):
        to = lax.rem(z + d, 8)
        return to, (lat, (to * 2 + xh) * 4 + y)

    def x_peer(d):
        to = lax.rem(x + d, 4)
        return to, (lax.rem(to, 2) * 2 + core, (z * 2 + to // 2) * 4 + y)

    def remote(src, dst, ss, rs, dev):
        return pltpu.make_async_remote_copy(
            src_ref=src, dst_ref=dst, send_sem=ss, recv_sem=rs, device_id=dev, device_id_type=MESH
        )

    bar = pltpu.get_barrier_semaphore()
    peers = [sib]
    for q in range(4):
        for side in (left, right):
            peers.append((q, side))
    peers += [((1 - xlo) * 2 + t, lon) for t in range(2)]
    peers += [y_peer(d)[1] for d in (1, 2, 3)]
    peers += [x_peer(d)[1] for d in (1, 2, 3)]
    peers += [z_peer(d)[1] for d in range(1, 8)]
    for p in peers:
        pl.semaphore_signal(bar, inc=1, device_id=p, device_id_type=MESH)

    own = 1 + 2 * core
    loads = [
        pltpu.make_async_copy(go_hbm, ext.at[pl.ds(own, 2), pl.ds(16, B)], ld_sem.at[0]),
        pltpu.make_async_copy(pre_hbm, pre_own, ld_sem.at[1]),
    ]
    for h in range(2):
        loads.append(
            pltpu.make_async_copy(
                pre_hbm.at[:, :, pl.ds(pl.multiple_of(core * 128, 128) + 256 * h, 128)],
                pre_half.at[pl.ds(2 * core, 2), :, pl.ds(128 * h, 128)],
                ld_sem.at[2 + h],
            )
        )
    for cp in loads:
        cp.start()
    w_loads = []
    for i in range(3):
        for j in range(3):
            cp = pltpu.make_async_copy(w_hbm.at[i, j], wv.at[i, :, pl.ds(512 * j, 512)], w_sem.at[3 * i + j])
            cp.start()
            w_loads.append(cp)

    pl.semaphore_wait(bar, len(peers))

    sib_copies = []
    for m in range(2):
        sib_copies.append(
            remote(go_hbm.at[m], ext.at[own + m, pl.ds(16, B)], sib_s.at[m], sib_r.at[m], sib)
        )
    for h in range(2):
        sib_copies.append(
            remote(
                pre_hbm.at[:, :, pl.ds(pl.multiple_of((1 - core) * 128, 128) + 256 * h, 128)],
                pre_half.at[pl.ds(2 * core, 2), :, pl.ds(128 * h, 128)],
                sib_s.at[2 + h], sib_r.at[2 + h], sib,
            )
        )
    rims = []
    for t in range(2):
        rims.append(
            remote(
                go_hbm.at[:, pl.ds(B - 16, 16)], ext.at[pl.ds(own, 2), pl.ds(0, 16)],
                rim_s.at[0, t], rim_r.at[0, core], (xlo * 2 + t, right),
            )
        )
        rims.append(
            remote(
                go_hbm.at[:, pl.ds(0, 16)], ext.at[pl.ds(own, 2), pl.ds(16 + B, 16)],
                rim_s.at[1, t], rim_r.at[1, core], (xlo * 2 + t, left),
            )
        )
    for cp in rims:
        cp.start()
    for cp in sib_copies:
        cp.start()

    owner = core + xlo == 1
    far = 5 * xlo
    halos = []
    for t in range(2):
        halos.append(
            remote(
                go_hbm.at[core, pl.ds(384 * t, 384)], ext.at[far, pl.ds(16 + 384 * t, 384)],
                halo_s.at[t], halo_r, ((1 - xlo) * 2 + t, lon),
            )
        )
        halos.append(
            remote(
                go_hbm.at[core, pl.ds(B - 16, 16)], ext.at[far, pl.ds(0, 16)],
                hrim_s.at[0, t], hrim_r.at[0], ((1 - xlo) * 2 + t, right),
            )
        )
        halos.append(
            remote(
                go_hbm.at[core, pl.ds(0, 16)], ext.at[far, pl.ds(16 + B, 16)],
                hrim_s.at[1, t], hrim_r.at[1], ((1 - xlo) * 2 + t, left),
            )
        )

    @pl.when(owner)
    def _():
        for cp in halos:
            cp.start()

    def spread(r):
        rows = pl.ds(pl.multiple_of(r * B, B), B)
        gos[rows, 0:512] = ext[r, 17 : 17 + B, :]
        gos[rows, 512:1024] = ext[r, 16 : 16 + B, :]
        gos[rows, 1024:1536] = ext[r, 15 : 15 + B, :]

    def activate(r):
        @pl.loop(0, 3)
        def _(n):
            v = pre_half[r, pl.ds(pl.multiple_of(n * 256, 256), 256), :].astype(F32)
            act[pl.ds(pl.multiple_of(r * B + n * 256, 256), 256), :] = (v * sigmoid(v)).astype(BF)

    zero_row = 5 * xlo
    gos[pl.ds(pl.multiple_of(zero_row * B, B), B), :] = jnp.zeros((B, 1536), BF)

    for cp in loads:
        cp.wait()

    @pl.loop(0, 2)
    def _(m):
        activate(2 * core + m)

    def wait_rims(cc):
        rows = pl.ds(1 + 2 * cc, 2)
        for side, at in ((0, 0), (1, 16 + B)):
            remote(
                ext.at[rows, pl.ds(at, 16)], ext.at[rows, pl.ds(at, 16)],
                rim_s.at[side, 0], rim_r.at[side, cc], sib,
            ).wait_recv()

    wait_rims(core)

    @pl.loop(0, 2)
    def _(m):
        spread(own + m)

    for cp in w_loads:
        cp.wait()

    @pl.loop(0, 6)
    def _(n):
        m, at = n // 3, lax.rem(n, 3) * 256

        def rows(r):
            return pl.ds(pl.multiple_of(r * B + at, 256), 256)

        here = lax.dot_general(gos[rows(own + m), :], wv[1], NT, preferred_element_type=F32)
        there = lax.dot_general(gos[rows(own + 1 - m), :], wv[2 * m], NT, preferred_element_type=F32)
        acc[pl.ds(pl.multiple_of(n * 256, 256), 256), :] = here + there

    other = 1 + 2 * (1 - core)
    for m in range(2):
        remote(
            ext.at[other + m, pl.ds(16, B)], ext.at[other + m, pl.ds(16, B)], sib_s.at[m], sib_r.at[m], sib
        ).wait_recv()
    for h in range(2):
        part = pre_half.at[pl.ds(2 * (1 - core), 2), :, pl.ds(128 * h, 128)]
        remote(part, part, sib_s.at[2 + h], sib_r.at[2 + h], sib).wait_recv()
    wait_rims(1 - core)

    @pl.loop(0, 2)
    def _(m):
        activate(2 * (1 - core) + m)
        spread(other + m)

    def term(j, g0, a0, k):
        return lax.dot_general(
            gos[pl.ds(pl.multiple_of(g0 * B, B), k), pl.ds(pl.multiple_of(j * 512, 512), 512)],
            act[pl.ds(pl.multiple_of(a0 * B, B), k), :],
            TN,
            preferred_element_type=F32,
        )

    def x_copy(j, d):
        to, dev = x_peer(d)
        return remote(send_x.at[j, to], recv_x.at[j, d - 1], x_s.at[j, d - 1], x_r.at[j, d - 1], dev)

    def y_copy(t, d):
        to, dev = y_peer(d)
        return remote(send_y.at[t, to], recv_y.at[t, d - 1], y_s.at[t, d - 1], y_r.at[t, d - 1], dev)

    @pl.loop(0, 3)
    def _(j):
        p = term(j, 1, 0, 4 * B).reshape(8, 2, 32, 256)
        px[j] = p
        for a in range(2):
            for b in range(2):
                send_x[j, 2 * a + b] = p[:, a, :, 128 * b : 128 * b + 128].reshape(256, 128).astype(BF)
        for d in (1, 2, 3):
            x_copy(j, d).start()

    def first_y(t, j, g0, a0, k):
        p = term(j, g0, a0, k).reshape(16, 4, 8, 256)
        py[t] = p
        for to in range(4):
            send_y[t, to] = p[:, to].reshape(128, 256).astype(BF)
        for d in (1, 2, 3):
            y_copy(t, d).start()

    @pl.loop(0, 3)
    def _(j):
        first_y(j, j, 1 + xlo, 1 - xlo, 3 * B)

    near = 5 * (1 - xlo)
    half = ext.at[near, pl.ds(pl.multiple_of(16 + 384 * core, 16), 384)]
    other_half = ext.at[near, pl.ds(pl.multiple_of(16 + 384 * (1 - core), 16), 384)]
    remote(half, half, halo_s.at[0], halo_r, sib).wait_recv()
    forward = remote(half, half, fwd_s, fwd_r, sib)
    forward.start()
    for side, at in ((0, 0), (1, 16 + B)):
        edge = ext.at[near, pl.ds(at, 16)]
        remote(edge, edge, hrim_s.at[side, 0], hrim_r.at[side], sib).wait_recv()
    remote(other_half, other_half, fwd_s, fwd_r, sib).wait_recv()
    spread(near)

    @pl.loop(0, 3)
    def _(j):
        first_y(3 + j, j, 2 * (1 - xlo), 0, 4 * B)

    @pl.loop(0, 6)
    def _(n):
        m, at = n // 3, lax.rem(n, 3) * 256
        src = pl.ds(pl.multiple_of((2 * core + 3 * m) * B + at, 256), 256)
        rest = lax.dot_general(gos[src, :], wv[2 - 2 * m], NT, preferred_element_type=F32)
        grad = acc[pl.ds(pl.multiple_of(n * 256, 256), 256), :] + rest
        cells = pl.ds(pl.multiple_of(at, 256), 256)
        h = pre_own[m, cells, :].astype(F32)
        s = sigmoid(h)
        gin[m, cells, :] = (grad * s * (1.0 + h * (1.0 - s))).astype(BF)

    store = pltpu.make_async_copy(gin, gin_hbm, out_sem)
    store.start()

    def z_copy(g, d):
        to, dev = z_peer(d)
        return remote(send_z.at[g, to], recv_z.at[g, d - 1], z_s.at[g, d - 1], z_r.at[g, d - 1], dev)

    def zx_copy(d):
        to, dev = z_peer(d)
        return remote(send_zx.at[to], recv_zx.at[d - 1], zx_s.at[d - 1], zx_r.at[d - 1], dev)

    def finish_y(g):
        @pl.loop(0, 3)
        def _(j):
            t = 3 * g + j
            total = py[t, :, y].reshape(128, 256)
            for d in (1, 2, 3):
                y_copy(t, d).wait_recv()
                total = total + recv_y[t, d - 1].astype(F32)
            total = total.reshape(8, 16, 256)
            zy[t] = total
            for to in range(8):
                send_z[g, to, j] = total[to].astype(BF)

        for d in range(1, 8):
            z_copy(g, d).start()

    def finish_x():
        @pl.loop(0, 3)
        def _(j):
            total = px[j, :, xh, :, pl.ds(pl.multiple_of(xlo * 128, 128), 128)].reshape(256, 128)
            for d in (1, 2, 3):
                x_copy(j, d).wait_recv()
                total = total + recv_x[j, d - 1].astype(F32)
            total = total.reshape(8, 32, 128)
            zx[j] = total
            for to in range(8):
                send_zx[to, j] = total[to].astype(BF)

        for d in range(1, 8):
            zx_copy(d).start()

    finish_y(0)
    finish_x()
    finish_y(1)

    def finish_z(g, slot):
        for d in range(1, 8):
            z_copy(g, d).wait_recv()

        @pl.loop(0, 3)
        def _(j):
            total = zy[3 * g + j, z]
            for d in range(1, 8):
                total = total + recv_z[g, d - 1, j].astype(F32)
            for a in range(2):
                for b in range(2):
                    send_xf[2 * a + b, slot, j] = total[8 * a : 8 * a + 8, 128 * b : 128 * b + 128]

    def yf_copy(d):
        to, dev = y_peer(d)
        return remote(send_yf.at[to], recv_yf.at[d - 1], yf_s.at[d - 1], yf_r.at[d - 1], dev)

    def xf_copy(d):
        to, dev = x_peer(d)
        return remote(send_xf.at[to], recv_xf.at[d - 1], xf_s.at[d - 1], xf_r.at[d - 1], dev)

    finish_z(0, 1 - xlo)
    for d in range(1, 8):
        zx_copy(d).wait_recv()

    @pl.loop(0, 3)
    def _(j):
        total = zx[j, z]
        for d in range(1, 8):
            total = total + recv_zx[d - 1, j].astype(F32)
        for to in range(4):
            send_yf[to, j] = total[8 * to : 8 * to + 8, :]

    for d in (1, 2, 3):
        yf_copy(d).start()
    finish_z(1, xlo)
    for d in (1, 2, 3):
        xf_copy(d).start()

    for d in (1, 2, 3):
        yf_copy(d).wait_recv()
    final[1] = send_yf[y] + recv_yf[0] + recv_yf[1] + recv_yf[2]
    for d in (1, 2, 3):
        xf_copy(d).wait_recv()
    for gi in range(2):
        final[2 * gi] = send_xf[x, gi] + recv_xf[0, gi] + recv_xf[1, gi] + recv_xf[2, gi]

    all_terms = final[...].reshape(9, 8, 128)
    total = jnp.sum(all_terms * all_terms, axis=0)
    ar_own[0] = total
    cp = remote(ar_own.at[0], ar_core, ar_s.at[0], ar_r.at[0], sib)
    cp.start()
    sums = [cp]
    cp.wait_recv()
    total = total + ar_core[...]
    at = 1
    for stage, (peer, count, slots) in enumerate(((y_peer, 3, ar_y), (x_peer, 3, ar_x), (z_peer, 7, ar_z))):
        ar_own[1 + stage] = total
        copies = []
        for d in range(1, count + 1):
            cp = remote(ar_own.at[1 + stage], slots.at[d - 1], ar_s.at[at], ar_r.at[at], peer(d)[1])
            at = at + 1
            cp.start()
            copies.append(cp)
        for cp in copies:
            cp.wait_recv()
        for d in range(count):
            total = total + slots[d]
        sums += copies
    grand = jnp.sum(total)
    factor = jnp.float32(3.0 * C) * lax.rsqrt(jnp.full((8, 128), grand, F32) + 1e-06)
    for i in range(3):
        for j in range(3):
            gk_ref[:, i, j, :] = final[i, j] * factor

    for cp in rims + sib_copies:
        cp.wait_send()

    @pl.when(owner)
    def _():
        for cp in halos:
            cp.wait_send()

    forward.wait_send()
    for d in (1, 2, 3):
        for j in range(3):
            x_copy(j, d).wait_send()
        for t in range(6):
            y_copy(t, d).wait_send()
        yf_copy(d).wait_send()
        xf_copy(d).wait_send()
    for d in range(1, 8):
        for g in range(2):
            z_copy(g, d).wait_send()
        zx_copy(d).wait_send()
    for cp in sums:
        cp.wait_send()
    store.wait()


def shards(pre_act, grad_out, kernel):
    vmem = pltpu.VMEM
    dma = pltpu.SemaphoreType.DMA
    scratch = [
        vmem((6, B + 32, C), BF),
        vmem((6 * B, 3 * C), BF),
        vmem((3, C, 3 * C), BF),
        vmem((4, B, 256), BF),
        vmem((2, B, C), BF),
        vmem((4 * B, 256), BF),
        vmem((2 * B, C), F32),
        vmem((2, B, C), BF),
        vmem((3, 8, 2, 32, 256), F32),
        vmem((3, 4, 256, 128), BF),
        vmem((3, 3, 256, 128), BF),
        vmem((3, 8, 32, 128), F32),
        vmem((8, 3, 32, 128), BF),
        vmem((7, 3, 32, 128), BF),
        vmem((4, 3, 8, 128), F32),
        vmem((3, 3, 8, 128), F32),
        vmem((6, 16, 4, 8, 256), F32),
        vmem((6, 4, 128, 256), BF),
        vmem((6, 3, 128, 256), BF),
        vmem((6, 8, 16, 256), F32),
        vmem((2, 8, 3, 16, 256), BF),
        vmem((2, 7, 3, 16, 256), BF),
        vmem((4, 2, 3, 8, 128), F32),
        vmem((3, 2, 3, 8, 128), F32),
        vmem((3, 3, 8, 128), F32),
        vmem((4, 8, 128), F32),
        vmem((8, 128), F32),
        vmem((3, 8, 128), F32),
        vmem((3, 8, 128), F32),
        vmem((7, 8, 128), F32),
        dma((4,)), dma((9,)), dma, dma((4,)), dma((4,)), dma((2, 2)), dma((2, 2)),
        dma((2,)), dma, dma((2, 2)), dma((2,)), dma, dma,
        dma((3, 3)), dma((3, 3)), dma((7,)), dma((7,)), dma((3,)), dma((3,)),
        dma((6, 3)), dma((6, 3)), dma((2, 7)), dma((2, 7)), dma((3,)), dma((3,)), dma((14,)), dma((14,)),
    ]
    return pl.pallas_call(
        body,
        out_shape=(
            jax.ShapeDtypeStruct((2, B, C), BF),
            jax.ShapeDtypeStruct((8, 3, 3, 128), F32),
        ),
        in_specs=[pl.BlockSpec(memory_space=pl.ANY)] * 3,
        out_specs=(pl.BlockSpec(memory_space=pl.ANY), pl.BlockSpec(memory_space=pltpu.VMEM)),
        scratch_shapes=scratch,
        compiler_params=pltpu.CompilerParams(
            collective_id=0, has_side_effects=True, vmem_limit_bytes=58 * 2**20
        ),
        cost_estimate=pl.CostEstimate(flops=14_500_000_000, bytes_accessed=12_000_000, transcendentals=1_600_000),
        name="conv_backward",
    )(pre_act, grad_out, kernel)


def solution(mesh):
    in_specs = (P("lat", "lon", None), P("lat", "lon", None), P())
    out_specs = (P("lat", "lon", None), P("lon", None, None, "lat"))
    return jax.shard_map(shards, mesh=mesh, in_specs=in_specs, out_specs=out_specs, check_vma=False)
```

```python
import jax
import jax.numpy as jnp
from jax import lax
from jax.experimental import pallas as pl
from jax.experimental.pallas import tpu as pltpu
from jax.sharding import PartitionSpec as P

BF = jnp.bfloat16
F32 = jnp.float32
MESH = pl.DeviceIdType.MESH
B = 768
C = 512
TN = (((0,), (0,)), ((), ()))
NT = (((1,), (1,)), ((), ()))


def sigmoid(v):
    return 1.0 / (1.0 + jnp.exp(-v))


def body(
    pre_hbm, go_hbm, w_hbm, gin_hbm, gk_ref,
    ext, gos, wv, pre_half, pre_own, act, acc, gin,
    px, send_x, recv_x, mx_own, send_my, recv_my,
    py, send_y, recv_y, my_own, send_mx, recv_mx,
    pz, send_z, recv_z, mz_own, send_mz, recv_mz,
    send_zf, recv_zf, send_xf, recv_xf,
    final, ar_own, ar_core, ar_y, ar_x, ar_z,
    ld_sem, w_sem, out_sem, sib_s, sib_r, rim_s, rim_r, halo_s, halo_r, hrim_s, hrim_r, fwd_s, fwd_r,
    x_s, x_r, my_s, my_r, y_s, y_r, mx_s, mx_r, z_s, z_r, mz_s, mz_r, zf_s, zf_r, xf_s, xf_r, ar_s, ar_r,
):
    lat = lax.axis_index("lat")
    lon = lax.axis_index("lon")
    xlo, core = lat // 2, lat % 2
    z, xh, y = lon // 8, (lon // 4) % 2, lon % 4
    x = xh * 2 + xlo

    sib = (xlo * 2 + 1 - core, lon)
    left, right = lax.rem(lon + 63, 64), lax.rem(lon + 1, 64)

    def y_peer(d):
        to = lax.rem(y + d, 4)
        return to, (lat, (z * 2 + xh) * 4 + to)

    def z_peer(d):
        to = lax.rem(z + d, 8)
        return to, (lat, (to * 2 + xh) * 4 + y)

    def x_peer(d):
        to = lax.rem(x + d, 4)
        return to, (lax.rem(to, 2) * 2 + core, (z * 2 + to // 2) * 4 + y)

    def remote(src, dst, ss, rs, dev):
        return pltpu.make_async_remote_copy(
            src_ref=src, dst_ref=dst, send_sem=ss, recv_sem=rs, device_id=dev, device_id_type=MESH
        )

    bar = pltpu.get_barrier_semaphore()
    peers = [sib]
    for q in range(4):
        for side in (left, right):
            peers.append((q, side))
    peers += [((1 - xlo) * 2 + t, lon) for t in range(2)]
    peers += [y_peer(d)[1] for d in (1, 2, 3)]
    peers += [x_peer(d)[1] for d in (1, 2, 3)]
    peers += [z_peer(d)[1] for d in range(1, 8)]
    for p in peers:
        pl.semaphore_signal(bar, inc=1, device_id=p, device_id_type=MESH)

    own = 1 + 2 * core
    loads = [
        pltpu.make_async_copy(go_hbm, ext.at[pl.ds(own, 2), pl.ds(16, B)], ld_sem.at[0]),
        pltpu.make_async_copy(pre_hbm, pre_own, ld_sem.at[1]),
    ]
    for h in range(2):
        loads.append(
            pltpu.make_async_copy(
                pre_hbm.at[:, :, pl.ds(pl.multiple_of(core * 128, 128) + 256 * h, 128)],
                pre_half.at[pl.ds(2 * core, 2), :, pl.ds(128 * h, 128)],
                ld_sem.at[2 + h],
            )
        )
    for cp in loads:
        cp.start()
    w_loads = []
    for i in range(3):
        for j in range(3):
            cp = pltpu.make_async_copy(w_hbm.at[i, j], wv.at[i, :, pl.ds(512 * j, 512)], w_sem.at[3 * i + j])
            cp.start()
            w_loads.append(cp)

    pl.semaphore_wait(bar, len(peers))

    sib_copies = []
    for m in range(2):
        sib_copies.append(
            remote(go_hbm.at[m], ext.at[own + m, pl.ds(16, B)], sib_s.at[m], sib_r.at[m], sib)
        )
    for h in range(2):
        sib_copies.append(
            remote(
                pre_hbm.at[:, :, pl.ds(pl.multiple_of((1 - core) * 128, 128) + 256 * h, 128)],
                pre_half.at[pl.ds(2 * core, 2), :, pl.ds(128 * h, 128)],
                sib_s.at[2 + h], sib_r.at[2 + h], sib,
            )
        )
    rims = []
    for t in range(2):
        rims.append(
            remote(
                go_hbm.at[:, pl.ds(B - 16, 16)], ext.at[pl.ds(own, 2), pl.ds(0, 16)],
                rim_s.at[0, t], rim_r.at[0, core], (xlo * 2 + t, right),
            )
        )
        rims.append(
            remote(
                go_hbm.at[:, pl.ds(0, 16)], ext.at[pl.ds(own, 2), pl.ds(16 + B, 16)],
                rim_s.at[1, t], rim_r.at[1, core], (xlo * 2 + t, left),
            )
        )
    for cp in rims:
        cp.start()
    for cp in sib_copies:
        cp.start()

    owner = core + xlo == 1
    far = 5 * xlo
    halos = []
    for t in range(2):
        halos.append(
            remote(
                go_hbm.at[core, pl.ds(384 * t, 384)], ext.at[far, pl.ds(16 + 384 * t, 384)],
                halo_s.at[t], halo_r, ((1 - xlo) * 2 + t, lon),
            )
        )
        halos.append(
            remote(
                go_hbm.at[core, pl.ds(B - 16, 16)], ext.at[far, pl.ds(0, 16)],
                hrim_s.at[0, t], hrim_r.at[0], ((1 - xlo) * 2 + t, right),
            )
        )
        halos.append(
            remote(
                go_hbm.at[core, pl.ds(0, 16)], ext.at[far, pl.ds(16 + B, 16)],
                hrim_s.at[1, t], hrim_r.at[1], ((1 - xlo) * 2 + t, left),
            )
        )

    @pl.when(owner)
    def _():
        for cp in halos:
            cp.start()

    def spread(r):
        rows = pl.ds(pl.multiple_of(r * B, B), B)
        gos[rows, 0:512] = ext[r, 17 : 17 + B, :]
        gos[rows, 512:1024] = ext[r, 16 : 16 + B, :]
        gos[rows, 1024:1536] = ext[r, 15 : 15 + B, :]

    def activate(r):
        @pl.loop(0, 3)
        def _(n):
            v = pre_half[r, pl.ds(pl.multiple_of(n * 256, 256), 256), :].astype(F32)
            act[pl.ds(pl.multiple_of(r * B + n * 256, 256), 256), :] = (v * sigmoid(v)).astype(BF)

    zero_row = 5 * xlo
    gos[pl.ds(pl.multiple_of(zero_row * B, B), B), :] = jnp.zeros((B, 1536), BF)

    for cp in loads:
        cp.wait()

    @pl.loop(0, 2)
    def _(m):
        activate(2 * core + m)

    def wait_rims(cc):
        rows = pl.ds(1 + 2 * cc, 2)
        for side, at in ((0, 0), (1, 16 + B)):
            remote(
                ext.at[rows, pl.ds(at, 16)], ext.at[rows, pl.ds(at, 16)],
                rim_s.at[side, 0], rim_r.at[side, cc], sib,
            ).wait_recv()

    wait_rims(core)

    @pl.loop(0, 2)
    def _(m):
        spread(own + m)

    def own_share(n):
        m, at = n // 3, lax.rem(n, 3) * 256

        def rows(r):
            return pl.ds(pl.multiple_of(r * B + at, 256), 256)

        here = lax.dot_general(gos[rows(own + m), :], wv[1], NT, preferred_element_type=F32)
        there = lax.dot_general(gos[rows(own + 1 - m), :], wv[2 * m], NT, preferred_element_type=F32)
        acc[pl.ds(pl.multiple_of(n * 256, 256), 256), :] = here + there

    other = 1 + 2 * (1 - core)
    for m in range(2):
        remote(
            ext.at[other + m, pl.ds(16, B)], ext.at[other + m, pl.ds(16, B)], sib_s.at[m], sib_r.at[m], sib
        ).wait_recv()
    for h in range(2):
        part = pre_half.at[pl.ds(2 * (1 - core), 2), :, pl.ds(128 * h, 128)]
        remote(part, part, sib_s.at[2 + h], sib_r.at[2 + h], sib).wait_recv()
    wait_rims(1 - core)

    @pl.loop(0, 2)
    def _(m):
        activate(2 * (1 - core) + m)
        spread(other + m)

    def term(j, g0, a0, k):
        return lax.dot_general(
            gos[pl.ds(pl.multiple_of(g0 * B, B), k), pl.ds(pl.multiple_of(j * 512, 512), 512)],
            act[pl.ds(pl.multiple_of(a0 * B, B), k), :],
            TN,
            preferred_element_type=F32,
        )

    def x_copy(j, d):
        to, dev = x_peer(d)
        return remote(send_x.at[j, to], recv_x.at[j, d - 1], x_s.at[j, d - 1], x_r.at[j, d - 1], dev)

    def y_copy(t, d):
        to, dev = y_peer(d)
        return remote(send_y.at[t, to], recv_y.at[t, d - 1], y_s.at[t, d - 1], y_r.at[t, d - 1], dev)

    def z_copy(g, d):
        to, dev = z_peer(d)
        return remote(send_z.at[g, to], recv_z.at[g, d - 1], z_s.at[g, d - 1], z_r.at[g, d - 1], dev)

    def first_x(j):
        p = term(j, 1, 0, 4 * B).reshape(8, 2, 32, 256)
        px[j] = p
        for a in range(2):
            for b in range(2):
                send_x[j, 2 * a + b] = p[:, a, :, 128 * b : 128 * b + 128].reshape(256, 128).astype(BF)
        for d in (1, 2, 3):
            x_copy(j, d).start()

    def first_y(t, j, g0, a0, k):
        p = term(j, g0, a0, k).reshape(16, 4, 8, 256)
        py[t] = p
        for to in range(4):
            send_y[t, to] = p[:, to].reshape(128, 256).astype(BF)
        for d in (1, 2, 3):
            y_copy(t, d).start()

    def first_z(g, j, g0, a0, k):
        p = term(j, g0, a0, k).reshape(8, 64, 256)
        pz[g] = p
        send_z[g] = p.astype(BF)
        for d in range(1, 8):
            z_copy(g, d).start()

    first_z(0, 2, 1 + xlo, 1 - xlo, 3 * B)

    @pl.loop(0, 2)
    def _(j):
        first_y(j, j, 1 + xlo, 1 - xlo, 3 * B)
        first_x(j)

    near = 5 * (1 - xlo)
    half = ext.at[near, pl.ds(pl.multiple_of(16 + 384 * core, 16), 384)]
    other_half = ext.at[near, pl.ds(pl.multiple_of(16 + 384 * (1 - core), 16), 384)]
    remote(half, half, halo_s.at[0], halo_r, sib).wait_recv()
    forward = remote(half, half, fwd_s, fwd_r, sib)
    forward.start()
    first_x(2)

    for side, at in ((0, 0), (1, 16 + B)):
        edge = ext.at[near, pl.ds(at, 16)]
        remote(edge, edge, hrim_s.at[side, 0], hrim_r.at[side], sib).wait_recv()
    remote(other_half, other_half, fwd_s, fwd_r, sib).wait_recv()
    spread(near)

    first_z(1, 2, 2 * (1 - xlo), 0, 4 * B)

    @pl.loop(0, 2)
    def _(j):
        first_y(2 + j, j, 2 * (1 - xlo), 0, 4 * B)

    for cp in w_loads:
        cp.wait()

    @pl.loop(0, 3)
    def _(n):
        own_share(n)

    def rest(n):
        m, at = n // 3, lax.rem(n, 3) * 256
        src = pl.ds(pl.multiple_of((2 * core + 3 * m) * B + at, 256), 256)
        other_row = lax.dot_general(gos[src, :], wv[2 - 2 * m], NT, preferred_element_type=F32)
        grad = acc[pl.ds(pl.multiple_of(n * 256, 256), 256), :] + other_row
        cells = pl.ds(pl.multiple_of(at, 256), 256)
        h = pre_own[m, cells, :].astype(F32)
        s = sigmoid(h)
        gin[m, cells, :] = (grad * s * (1.0 + h * (1.0 - s))).astype(BF)

    store = pltpu.make_async_copy(gin, gin_hbm, out_sem)

    def my_copy(d):
        to, dev = y_peer(d)
        return remote(send_my.at[to], recv_my.at[d - 1], my_s.at[d - 1], my_r.at[d - 1], dev)

    def mx_copy(gi, d):
        to, dev = x_peer(d)
        return remote(send_mx.at[to, gi], recv_mx.at[d - 1, gi], mx_s.at[gi, d - 1], mx_r.at[gi, d - 1], dev)

    def mz_copy(g, d):
        to, dev = y_peer(d)
        return remote(send_mz.at[g, to], recv_mz.at[g, d - 1], mz_s.at[g, d - 1], mz_r.at[g, d - 1], dev)

    my_lanes = pl.ds(pl.multiple_of(xlo * 128, 128), 128)

    def finish_x():
        @pl.loop(0, 3)
        def _(j):
            total = px[j, :, xh, :, my_lanes].reshape(256, 128)
            for d in (1, 2, 3):
                x_copy(j, d).wait_recv()
                total = total + recv_x[j, d - 1].astype(F32)
            total = total.reshape(8, 4, 8, 128)
            mx_own[j] = total
            for to in range(4):
                send_my[to, j] = total[:, to].reshape(64, 128).astype(BF)

        for d in (1, 2, 3):
            my_copy(d).start()

    def finish_y(g, gi):
        @pl.loop(0, 2)
        def _(j):
            t = 2 * g + j
            total = py[t, :, y].reshape(128, 256)
            for d in (1, 2, 3):
                y_copy(t, d).wait_recv()
                total = total + recv_y[t, d - 1].astype(F32)
            total = total.reshape(8, 2, 8, 256)
            my_own[gi, j] = total
            for a in range(2):
                for b in range(2):
                    part = total[:, a, :, 128 * b : 128 * b + 128]
                    send_mx[2 * a + b, gi, j] = part.reshape(64, 128).astype(BF)

        for d in (1, 2, 3):
            mx_copy(gi, d).start()

    def finish_z(g):
        total = pz[g, z]
        for d in range(1, 8):
            z_copy(g, d).wait_recv()
            total = total + recv_z[g, d - 1].astype(F32)
        total = total.reshape(2, 4, 8, 256)
        mz_own[g] = total
        for to in range(4):
            send_mz[g, to] = total[:, to].reshape(16, 256).astype(BF)
        for d in (1, 2, 3):
            mz_copy(g, d).start()

    finish_x()
    finish_z(0)
    finish_y(0, 1 - xlo)

    @pl.loop(3, 6)
    def _(n):
        own_share(n)

    def zf_copy(part, d):
        to, dev = z_peer(d)
        which = (pl.ds(0, 3), pl.ds(3, 4))[part]
        return remote(
            send_zf.at[to, which], recv_zf.at[d - 1, which], zf_s.at[part, d - 1], zf_r.at[part, d - 1], dev
        )

    def xf_copy(d):
        to, dev = x_peer(d)
        return remote(send_xf.at[to], recv_xf.at[d - 1], xf_s.at[d - 1], xf_r.at[d - 1], dev)

    for d in (1, 2, 3):
        my_copy(d).wait_recv()

    @pl.loop(0, 3)
    def _(j):
        total = mx_own[j, :, y].reshape(64, 128)
        for d in range(3):
            total = total + recv_my[d, j].astype(F32)
        send_zf[:, j] = total.reshape(8, 8, 128)

    for d in range(1, 8):
        zf_copy(0, d).start()

    finish_z(1)
    finish_y(1, xlo)

    @pl.loop(0, 3)
    def _(n):
        rest(n)

    for g in range(2):
        slot = (1 - xlo, xlo)[g]
        total = mz_own[g, :, y].reshape(16, 256)
        for d in (1, 2, 3):
            mz_copy(g, d).wait_recv()
            total = total + recv_mz[g, d - 1].astype(F32)
        for a in range(2):
            for b in range(2):
                send_xf[2 * a + b, slot] = total[8 * a : 8 * a + 8, 128 * b : 128 * b + 128]
    for d in (1, 2, 3):
        xf_copy(d).start()

    for gi in range(2):
        for d in (1, 2, 3):
            mx_copy(gi, d).wait_recv()
        for j in range(2):
            total = my_own[gi, j, :, xh, :, my_lanes].reshape(64, 128)
            for d in range(3):
                total = total + recv_mx[d, gi, j].astype(F32)
            send_zf[:, 3 + 2 * gi + j] = total.reshape(8, 8, 128)
    for d in range(1, 8):
        zf_copy(1, d).start()

    @pl.loop(3, 6)
    def _(n):
        rest(n)

    store.start()

    for d in (1, 2, 3):
        xf_copy(d).wait_recv()
    for gi in range(2):
        final[2 * gi, 2] = send_xf[x, gi] + recv_xf[0, gi] + recv_xf[1, gi] + recv_xf[2, gi]
    for part in range(2):
        total = send_zf[z, pl.ds(3 * part, 3 + part)]
        for d in range(1, 8):
            zf_copy(part, d).wait_recv()
            total = total + recv_zf[d - 1, pl.ds(3 * part, 3 + part)]
        if part == 0:
            final[1] = total
        else:
            for gi in range(2):
                final[2 * gi, 0:2] = total[2 * gi : 2 * gi + 2]

    all_terms = final[...].reshape(9, 8, 128)
    total = jnp.sum(all_terms * all_terms, axis=0)
    ar_own[0] = total
    cp = remote(ar_own.at[0], ar_core, ar_s.at[0], ar_r.at[0], sib)
    cp.start()
    sums = [cp]
    cp.wait_recv()
    total = total + ar_core[...]
    at = 1
    for stage, (peer, count, slots) in enumerate(((y_peer, 3, ar_y), (x_peer, 3, ar_x), (z_peer, 7, ar_z))):
        ar_own[1 + stage] = total
        copies = []
        for d in range(1, count + 1):
            cp = remote(ar_own.at[1 + stage], slots.at[d - 1], ar_s.at[at], ar_r.at[at], peer(d)[1])
            at = at + 1
            cp.start()
            copies.append(cp)
        for cp in copies:
            cp.wait_recv()
        for d in range(count):
            total = total + slots[d]
        sums += copies
    grand = jnp.sum(total)
    factor = jnp.float32(3.0 * C) * lax.rsqrt(jnp.full((8, 128), grand, F32) + 1e-06)
    for i in range(3):
        for j in range(3):
            gk_ref[i, j] = final[i, j] * factor

    for cp in rims + sib_copies:
        cp.wait_send()

    @pl.when(owner)
    def _():
        for cp in halos:
            cp.wait_send()

    forward.wait_send()
    for d in (1, 2, 3):
        for j in range(3):
            x_copy(j, d).wait_send()
        for t in range(4):
            y_copy(t, d).wait_send()
        for g in range(2):
            mx_copy(g, d).wait_send()
            mz_copy(g, d).wait_send()
        my_copy(d).wait_send()
        xf_copy(d).wait_send()
    for d in range(1, 8):
        for g in range(2):
            z_copy(g, d).wait_send()
            zf_copy(g, d).wait_send()
    for cp in sums:
        cp.wait_send()
    store.wait()


def shards(pre_act, grad_out, kernel):
    vmem = pltpu.VMEM
    dma = pltpu.SemaphoreType.DMA
    scratch = [
        vmem((6, B + 32, C), BF),
        vmem((6 * B, 3 * C), BF),
        vmem((3, C, 3 * C), BF),
        vmem((4, B, 256), BF),
        vmem((2, B, C), BF),
        vmem((4 * B, 256), BF),
        vmem((2 * B, C), F32),
        vmem((2, B, C), BF),
        vmem((3, 8, 2, 32, 256), F32),
        vmem((3, 4, 256, 128), BF),
        vmem((3, 3, 256, 128), BF),
        vmem((3, 8, 4, 8, 128), F32),
        vmem((4, 3, 64, 128), BF),
        vmem((3, 3, 64, 128), BF),
        vmem((4, 16, 4, 8, 256), F32),
        vmem((4, 4, 128, 256), BF),
        vmem((4, 3, 128, 256), BF),
        vmem((2, 2, 8, 2, 8, 256), F32),
        vmem((4, 2, 2, 64, 128), BF),
        vmem((3, 2, 2, 64, 128), BF),
        vmem((2, 8, 64, 256), F32),
        vmem((2, 8, 64, 256), BF),
        vmem((2, 7, 64, 256), BF),
        vmem((2, 2, 4, 8, 256), F32),
        vmem((2, 4, 16, 256), BF),
        vmem((2, 3, 16, 256), BF),
        vmem((8, 7, 8, 128), F32),
        vmem((7, 7, 8, 128), F32),
        vmem((4, 2, 8, 128), F32),
        vmem((3, 2, 8, 128), F32),
        vmem((3, 3, 8, 128), F32),
        vmem((4, 8, 128), F32),
        vmem((8, 128), F32),
        vmem((3, 8, 128), F32),
        vmem((3, 8, 128), F32),
        vmem((7, 8, 128), F32),
        dma((4,)), dma((9,)), dma, dma((4,)), dma((4,)), dma((2, 2)), dma((2, 2)),
        dma((2,)), dma, dma((2, 2)), dma((2,)), dma, dma,
        dma((3, 3)), dma((3, 3)), dma((3,)), dma((3,)),
        dma((4, 3)), dma((4, 3)), dma((2, 3)), dma((2, 3)),
        dma((2, 7)), dma((2, 7)), dma((2, 3)), dma((2, 3)),
        dma((2, 7)), dma((2, 7)), dma((3,)), dma((3,)), dma((14,)), dma((14,)),
    ]
    grad_in, grad_kernel = pl.pallas_call(
        body,
        out_shape=(
            jax.ShapeDtypeStruct((2, B, C), BF),
            jax.ShapeDtypeStruct((3, 3, 8, 128), F32),
        ),
        in_specs=[pl.BlockSpec(memory_space=pl.ANY)] * 3,
        out_specs=(pl.BlockSpec(memory_space=pl.ANY), pl.BlockSpec(memory_space=pltpu.VMEM)),
        scratch_shapes=scratch,
        compiler_params=pltpu.CompilerParams(
            collective_id=0, has_side_effects=True, vmem_limit_bytes=52 * 2**20
        ),
        cost_estimate=pl.CostEstimate(flops=14_500_000_000, bytes_accessed=12_000_000, transcendentals=1_600_000),
        name="conv_backward",
    )(pre_act, grad_out, kernel)
    return grad_in, jnp.transpose(grad_kernel, (2, 0, 1, 3))


def solution(mesh):
    in_specs = (P("lat", "lon", None), P("lat", "lon", None), P())
    out_specs = (P("lat", "lon", None), P("lon", None, None, "lat"))
    return jax.shard_map(shards, mesh=mesh, in_specs=in_specs, out_specs=out_specs, check_vma=False)
```

```python
import jax
import jax.numpy as jnp
from jax import lax
from jax.experimental import pallas as pl
from jax.experimental.pallas import tpu as pltpu
from jax.sharding import PartitionSpec as P

BF = jnp.bfloat16
F32 = jnp.float32
MESH = pl.DeviceIdType.MESH
B = 768
C = 512
TN = (((0,), (0,)), ((), ()))
NT = (((1,), (1,)), ((), ()))


def sigmoid(v):
    return 1.0 / (1.0 + jnp.exp(-v))


def body(
    pre_hbm, go_hbm, w_hbm, gin_hbm, gk_ref,
    ext, gos, wv, pre_half, pre_own, act, acc, gin,
    px, send_x, recv_x, mx_own, send_my, recv_my,
    py, send_y, recv_y, my_own, send_mx, recv_mx,
    pz, send_z, recv_z, mz_own, send_mz, recv_mz,
    send_zf, recv_zf, send_xf, recv_xf,
    final, ar_own, ar_core, ar_xy, ar_z,
    ld_sem, w_sem, out_sem, sib_s, sib_r, rim_s, rim_r, halo_s, halo_r, hrim_s, hrim_r, fwd_s, fwd_r,
    x_s, x_r, my_s, my_r, y_s, y_r, mx_s, mx_r, z_s, z_r, mz_s, mz_r, zf_s, zf_r, xf_s, xf_r, ar_s, ar_r,
):
    lat = lax.axis_index("lat")
    lon = lax.axis_index("lon")
    xlo, core = lat // 2, lat % 2
    z, xh, y = lon // 8, (lon // 4) % 2, lon % 4
    x = xh * 2 + xlo

    sib = (xlo * 2 + 1 - core, lon)
    left, right = lax.rem(lon + 63, 64), lax.rem(lon + 1, 64)

    def y_peer(d):
        to = lax.rem(y + d, 4)
        return to, (lat, (z * 2 + xh) * 4 + to)

    def z_peer(d):
        to = lax.rem(z + d, 8)
        return to, (lat, (to * 2 + xh) * 4 + y)

    def x_peer(d):
        to = lax.rem(x + d, 4)
        return to, (lax.rem(to, 2) * 2 + core, (z * 2 + to // 2) * 4 + y)

    def plane_peer(d):
        tx, ty = lax.rem(x + d % 4, 4), lax.rem(y + d // 4, 4)
        return tx * 4 + ty, (lax.rem(tx, 2) * 2 + core, (z * 2 + tx // 2) * 4 + ty)

    def remote(src, dst, ss, rs, dev):
        return pltpu.make_async_remote_copy(
            src_ref=src, dst_ref=dst, send_sem=ss, recv_sem=rs, device_id=dev, device_id_type=MESH
        )

    bar = pltpu.get_barrier_semaphore()
    peers = [z_peer(d)[1] for d in (4, 3, 5, 2, 6, 1, 7)]
    for side in (left, right):
        for q in range(4):
            peers.append((q, side))
    peers += [plane_peer(d)[1] for d in range(1, 16)]
    peers += [((1 - xlo) * 2 + t, lon) for t in range(2)]
    peers.append(sib)
    for p in peers:
        pl.semaphore_signal(bar, inc=1, device_id=p, device_id_type=MESH)

    own = 1 + 2 * core
    loads = [
        pltpu.make_async_copy(go_hbm, ext.at[pl.ds(own, 2), pl.ds(16, B)], ld_sem.at[0]),
        pltpu.make_async_copy(pre_hbm, pre_own, ld_sem.at[1]),
    ]
    for h in range(2):
        loads.append(
            pltpu.make_async_copy(
                pre_hbm.at[:, :, pl.ds(pl.multiple_of(core * 128, 128) + 256 * h, 128)],
                pre_half.at[pl.ds(2 * core, 2), :, pl.ds(128 * h, 128)],
                ld_sem.at[2 + h],
            )
        )
    for cp in loads:
        cp.start()
    pl.semaphore_wait(bar, len(peers))

    sib_copies = []
    for m in range(2):
        sib_copies.append(
            remote(go_hbm.at[m], ext.at[own + m, pl.ds(16, B)], sib_s.at[m], sib_r.at[m], sib)
        )
    for h in range(2):
        sib_copies.append(
            remote(
                pre_hbm.at[:, :, pl.ds(pl.multiple_of((1 - core) * 128, 128) + 256 * h, 128)],
                pre_half.at[pl.ds(2 * core, 2), :, pl.ds(128 * h, 128)],
                sib_s.at[2 + h], sib_r.at[2 + h], sib,
            )
        )
    rims = []
    for t in range(2):
        rims.append(
            remote(
                go_hbm.at[:, pl.ds(B - 16, 16)], ext.at[pl.ds(own, 2), pl.ds(0, 16)],
                rim_s.at[0, t], rim_r.at[0, core], (xlo * 2 + t, right),
            )
        )
        rims.append(
            remote(
                go_hbm.at[:, pl.ds(0, 16)], ext.at[pl.ds(own, 2), pl.ds(16 + B, 16)],
                rim_s.at[1, t], rim_r.at[1, core], (xlo * 2 + t, left),
            )
        )
    for cp in rims:
        cp.start()
    for cp in sib_copies:
        cp.start()

    owner = core + xlo == 1
    far = 5 * xlo
    halos = []
    for t in range(2):
        halos.append(
            remote(
                go_hbm.at[core, pl.ds(384 * t, 384)], ext.at[far, pl.ds(16 + 384 * t, 384)],
                halo_s.at[t], halo_r, ((1 - xlo) * 2 + t, lon),
            )
        )
        halos.append(
            remote(
                go_hbm.at[core, pl.ds(B - 16, 16)], ext.at[far, pl.ds(0, 16)],
                hrim_s.at[0, t], hrim_r.at[0], ((1 - xlo) * 2 + t, right),
            )
        )
        halos.append(
            remote(
                go_hbm.at[core, pl.ds(0, 16)], ext.at[far, pl.ds(16 + B, 16)],
                hrim_s.at[1, t], hrim_r.at[1], ((1 - xlo) * 2 + t, left),
            )
        )

    @pl.when(owner)
    def _():
        for cp in halos:
            cp.start()

    w_loads = []
    for i in range(3):
        for j in range(3):
            cp = pltpu.make_async_copy(w_hbm.at[i, j], wv.at[i, :, pl.ds(512 * j, 512)], w_sem.at[3 * i + j])
            cp.start()
            w_loads.append(cp)

    def centre(r):
        gos[pl.ds(pl.multiple_of(r * B, B), B), 512:1024] = ext[r, 16 : 16 + B, :]

    def sides(r):
        rows = pl.ds(pl.multiple_of(r * B, B), B)
        gos[rows, 0:512] = ext[r, 17 : 17 + B, :]
        gos[rows, 1024:1536] = ext[r, 15 : 15 + B, :]

    def activate(r):
        @pl.loop(0, 3)
        def _(n):
            v = pre_half[r, pl.ds(pl.multiple_of(n * 256, 256), 256), :].astype(F32)
            act[pl.ds(pl.multiple_of(r * B + n * 256, 256), 256), :] = (v * sigmoid(v)).astype(BF)

    zero_row = 5 * xlo
    gos[pl.ds(pl.multiple_of(zero_row * B, B), B), :] = jnp.zeros((B, 1536), BF)

    for cp in loads:
        cp.wait()

    @pl.loop(0, 2)
    def _(m):
        activate(2 * core + m)
        centre(own + m)

    def wait_rims(cc):
        rows = pl.ds(1 + 2 * cc, 2)
        for side, at in ((0, 0), (1, 16 + B)):
            remote(
                ext.at[rows, pl.ds(at, 16)], ext.at[rows, pl.ds(at, 16)],
                rim_s.at[side, 0], rim_r.at[side, cc], sib,
            ).wait_recv()

    def term(j, g0, a0, k):
        return lax.dot_general(
            gos[pl.ds(pl.multiple_of(g0 * B, B), k), pl.ds(pl.multiple_of(j * 512, 512), 512)],
            act[pl.ds(pl.multiple_of(a0 * B, B), k), :],
            TN,
            preferred_element_type=F32,
        )

    def own_rows(j):
        px[j] = term(j, own, 2 * core, 2 * B).reshape(8, 2, 32, 256)

    def own_pair(j):
        return term(j, own + xlo, 2 * core + 1 - xlo, B)

    own_rows(1)
    py[1] = own_pair(1).reshape(16, 4, 8, 256)

    wait_rims(core)

    @pl.loop(0, 2)
    def _(m):
        sides(own + m)

    py[0] = own_pair(0).reshape(16, 4, 8, 256)
    pz[0] = own_pair(2).reshape(8, 64, 256)

    @pl.loop(0, 2)
    def _(n):
        own_rows(2 * n)

    other = 1 + 2 * (1 - core)
    for m in range(2):
        remote(
            ext.at[other + m, pl.ds(16, B)], ext.at[other + m, pl.ds(16, B)], sib_s.at[m], sib_r.at[m], sib
        ).wait_recv()
    for h in range(2):
        part = pre_half.at[pl.ds(2 * (1 - core), 2), :, pl.ds(128 * h, 128)]
        remote(part, part, sib_s.at[2 + h], sib_r.at[2 + h], sib).wait_recv()
    wait_rims(1 - core)

    @pl.loop(0, 2)
    def _(m):
        activate(2 * (1 - core) + m)
        centre(other + m)
        sides(other + m)

    def x_copy(j, d):
        to, dev = x_peer(d)
        return remote(send_x.at[j, to], recv_x.at[j, d - 1], x_s.at[j, d - 1], x_r.at[j, d - 1], dev)

    def y_copy(t, d):
        to, dev = y_peer(d)
        return remote(send_y.at[t, to], recv_y.at[t, d - 1], y_s.at[t, d - 1], y_r.at[t, d - 1], dev)

    def z_copy(g, d):
        to, dev = z_peer(d)
        return remote(send_z.at[g, to], recv_z.at[g, d - 1], z_s.at[g, d - 1], z_r.at[g, d - 1], dev)

    def first_x(j):
        p = px[j] + term(j, other, 2 * (1 - core), 2 * B).reshape(8, 2, 32, 256)
        px[j] = p
        for a in range(2):
            for b in range(2):
                send_x[j, 2 * a + b] = p[:, a, :, 128 * b : 128 * b + 128].reshape(256, 128).astype(BF)
        for d in (1, 2, 3):
            x_copy(j, d).start()

    def first_y(t, j, g0, a0, k):
        p = py[t] + term(j, g0, a0, k).reshape(16, 4, 8, 256)
        py[t] = p
        for to in range(4):
            send_y[t, to] = p[:, to].reshape(128, 256).astype(BF)
        for d in (1, 2, 3):
            y_copy(t, d).start()

    def first_z(g, j, g0, a0, k):
        p = pz[g] + term(j, g0, a0, k).reshape(8, 64, 256)
        pz[g] = p
        send_z[g] = p.astype(BF)
        for d in range(1, 8):
            z_copy(g, d).start()

    @pl.loop(0, 2)
    def _(j):
        first_y(j, j, 2 - core + xlo, 2 - core - xlo, 2 * B)

    first_z(0, 2, 2 - core + xlo, 2 - core - xlo, 2 * B)
    first_x(0)

    near = 5 * (1 - xlo)
    half = ext.at[near, pl.ds(pl.multiple_of(16 + 384 * core, 16), 384)]
    other_half = ext.at[near, pl.ds(pl.multiple_of(16 + 384 * (1 - core), 16), 384)]
    remote(half, half, halo_s.at[0], halo_r, sib).wait_recv()
    forward = remote(half, half, fwd_s, fwd_r, sib)
    forward.start()

    first_x(1)

    def local_pairs(j):
        return term(j, 2 - xlo, xlo, 3 * B)

    pz[1] = local_pairs(2).reshape(8, 64, 256)

    @pl.loop(0, 2)
    def _(j):
        py[2 + j] = local_pairs(j).reshape(16, 4, 8, 256)

    for side, at in ((0, 0), (1, 16 + B)):
        edge = ext.at[near, pl.ds(at, 16)]
        remote(edge, edge, hrim_s.at[side, 0], hrim_r.at[side], sib).wait_recv()
    remote(other_half, other_half, fwd_s, fwd_r, sib).wait_recv()
    centre(near)
    sides(near)

    @pl.loop(0, 2)
    def _(j):
        first_y(2 + j, j, near, 3 * (1 - xlo), B)

    first_z(1, 2, near, 3 * (1 - xlo), B)
    first_x(2)

    for cp in w_loads:
        cp.wait()

    def own_share(n):
        m, at = n // 3, lax.rem(n, 3) * 256

        def rows(r):
            return pl.ds(pl.multiple_of(r * B + at, 256), 256)

        here = lax.dot_general(gos[rows(own + m), :], wv[1], NT, preferred_element_type=F32)
        there = lax.dot_general(gos[rows(own + 1 - m), :], wv[2 * m], NT, preferred_element_type=F32)
        acc[pl.ds(pl.multiple_of(n * 256, 256), 256), :] = here + there

    @pl.loop(0, 3)
    def _(n):
        own_share(n)

    def rest(n):
        m, at = n // 3, lax.rem(n, 3) * 256
        src = pl.ds(pl.multiple_of((2 * core + 3 * m) * B + at, 256), 256)
        other_row = lax.dot_general(gos[src, :], wv[2 - 2 * m], NT, preferred_element_type=F32)
        grad = acc[pl.ds(pl.multiple_of(n * 256, 256), 256), :] + other_row
        cells = pl.ds(pl.multiple_of(at, 256), 256)
        h = pre_own[m, cells, :].astype(F32)
        s = sigmoid(h)
        gin[m, cells, :] = (grad * s * (1.0 + h * (1.0 - s))).astype(BF)

    store = pltpu.make_async_copy(gin, gin_hbm, out_sem)

    def my_copy(d):
        to, dev = y_peer(d)
        return remote(send_my.at[to], recv_my.at[d - 1], my_s.at[d - 1], my_r.at[d - 1], dev)

    def mx_copy(gi, d):
        to, dev = x_peer(d)
        return remote(send_mx.at[to, gi], recv_mx.at[d - 1, gi], mx_s.at[gi, d - 1], mx_r.at[gi, d - 1], dev)

    def mz_copy(g, d):
        to, dev = y_peer(d)
        return remote(send_mz.at[g, to], recv_mz.at[g, d - 1], mz_s.at[g, d - 1], mz_r.at[g, d - 1], dev)

    my_lanes = pl.ds(pl.multiple_of(xlo * 128, 128), 128)

    def finish_x():
        @pl.loop(0, 3)
        def _(j):
            total = px[j, :, xh, :, my_lanes].reshape(256, 128)
            for d in (1, 2, 3):
                x_copy(j, d).wait_recv()
                total = total + recv_x[j, d - 1].astype(F32)
            total = total.reshape(8, 4, 8, 128)
            mx_own[j] = total
            for to in range(4):
                send_my[to, j] = total[:, to].reshape(64, 128).astype(BF)

        for d in (1, 2, 3):
            my_copy(d).start()

    def finish_y(g, gi):
        @pl.loop(0, 2)
        def _(j):
            t = 2 * g + j
            total = py[t, :, y].reshape(128, 256)
            for d in (1, 2, 3):
                y_copy(t, d).wait_recv()
                total = total + recv_y[t, d - 1].astype(F32)
            total = total.reshape(8, 2, 8, 256)
            my_own[gi, j] = total
            for a in range(2):
                for b in range(2):
                    part = total[:, a, :, 128 * b : 128 * b + 128]
                    send_mx[2 * a + b, gi, j] = part.reshape(64, 128).astype(BF)

        for d in (1, 2, 3):
            mx_copy(gi, d).start()

    def finish_z(g):
        total = pz[g, z]
        for d in range(1, 8):
            z_copy(g, d).wait_recv()
            total = total + recv_z[g, d - 1].astype(F32)
        total = total.reshape(2, 4, 8, 256)
        mz_own[g] = total
        for to in range(4):
            send_mz[g, to] = total[:, to].reshape(16, 256).astype(BF)
        for d in (1, 2, 3):
            mz_copy(g, d).start()

    finish_x()
    finish_z(0)
    finish_y(0, 1 - xlo)

    @pl.loop(3, 6)
    def _(n):
        own_share(n)

    def zf_copy(part, d):
        to, dev = z_peer(d)
        which = (pl.ds(0, 3), pl.ds(3, 4))[part]
        return remote(
            send_zf.at[to, which], recv_zf.at[d - 1, which], zf_s.at[part, d - 1], zf_r.at[part, d - 1], dev
        )

    def xf_copy(d):
        to, dev = x_peer(d)
        return remote(send_xf.at[to], recv_xf.at[d - 1], xf_s.at[d - 1], xf_r.at[d - 1], dev)

    for d in (1, 2, 3):
        my_copy(d).wait_recv()

    @pl.loop(0, 3)
    def _(j):
        total = mx_own[j, :, y].reshape(64, 128)
        for d in range(3):
            total = total + recv_my[d, j].astype(F32)
        send_zf[:, j] = total.reshape(8, 8, 128)

    for d in range(1, 8):
        zf_copy(0, d).start()

    finish_z(1)
    finish_y(1, xlo)

    @pl.loop(0, 3)
    def _(n):
        rest(n)

    for g in range(2):
        slot = (1 - xlo, xlo)[g]
        total = mz_own[g, :, y].reshape(16, 256)
        for d in (1, 2, 3):
            mz_copy(g, d).wait_recv()
            total = total + recv_mz[g, d - 1].astype(F32)
        for a in range(2):
            for b in range(2):
                send_xf[2 * a + b, slot] = total[8 * a : 8 * a + 8, 128 * b : 128 * b + 128]
    for d in (1, 2, 3):
        xf_copy(d).start()

    for gi in range(2):
        for d in (1, 2, 3):
            mx_copy(gi, d).wait_recv()
        for j in range(2):
            total = my_own[gi, j, :, xh, :, my_lanes].reshape(64, 128)
            for d in range(3):
                total = total + recv_mx[d, gi, j].astype(F32)
            send_zf[:, 3 + 2 * gi + j] = total.reshape(8, 8, 128)
    for d in range(1, 8):
        zf_copy(1, d).start()

    @pl.loop(3, 6)
    def _(n):
        rest(n)

    store.start()

    for d in (1, 2, 3):
        xf_copy(d).wait_recv()
    for gi in range(2):
        final[2 * gi, 2] = send_xf[x, gi] + recv_xf[0, gi] + recv_xf[1, gi] + recv_xf[2, gi]
    for part in range(2):
        total = send_zf[z, pl.ds(3 * part, 3 + part)]
        for d in range(1, 8):
            zf_copy(part, d).wait_recv()
            total = total + recv_zf[d - 1, pl.ds(3 * part, 3 + part)]
        if part == 0:
            final[1] = total
        else:
            for gi in range(2):
                final[2 * gi, 0:2] = total[2 * gi : 2 * gi + 2]

    all_terms = final[...].reshape(9, 8, 128)
    total = jnp.sum(all_terms * all_terms, axis=0)
    ar_own[0] = total
    cp = remote(ar_own.at[0], ar_core, ar_s.at[0], ar_r.at[0], sib)
    cp.start()
    sums = [cp]
    cp.wait_recv()
    total = total + ar_core[...]
    at = 1
    for stage, (peer, count, slots) in enumerate(((plane_peer, 15, ar_xy), (z_peer, 7, ar_z))):
        ar_own[1 + stage] = total
        copies = []
        for d in range(1, count + 1):
            cp = remote(ar_own.at[1 + stage], slots.at[d - 1], ar_s.at[at], ar_r.at[at], peer(d)[1])
            at = at + 1
            cp.start()
            copies.append(cp)
        for cp in copies:
            cp.wait_recv()
        for d in range(count):
            total = total + slots[d]
        sums += copies
    grand = jnp.sum(total)
    factor = jnp.float32(3.0 * C) * lax.rsqrt(jnp.full((8, 128), grand, F32) + 1e-06)
    for i in range(3):
        for j in range(3):
            gk_ref[i, j] = final[i, j] * factor

    for cp in rims + sib_copies:
        cp.wait_send()

    @pl.when(owner)
    def _():
        for cp in halos:
            cp.wait_send()

    forward.wait_send()
    for d in (1, 2, 3):
        for j in range(3):
            x_copy(j, d).wait_send()
        for t in range(4):
            y_copy(t, d).wait_send()
        for g in range(2):
            mx_copy(g, d).wait_send()
            mz_copy(g, d).wait_send()
        my_copy(d).wait_send()
        xf_copy(d).wait_send()
    for d in range(1, 8):
        for g in range(2):
            z_copy(g, d).wait_send()
            zf_copy(g, d).wait_send()
    for cp in sums:
        cp.wait_send()
    store.wait()


def shards(pre_act, grad_out, kernel):
    vmem = pltpu.VMEM
    dma = pltpu.SemaphoreType.DMA
    scratch = [
        vmem((6, B + 32, C), BF),
        vmem((6 * B, 3 * C), BF),
        vmem((3, C, 3 * C), BF),
        vmem((4, B, 256), BF),
        vmem((2, B, C), BF),
        vmem((4 * B, 256), BF),
        vmem((2 * B, C), F32),
        vmem((2, B, C), BF),
        vmem((3, 8, 2, 32, 256), F32),
        vmem((3, 4, 256, 128), BF),
        vmem((3, 3, 256, 128), BF),
        vmem((3, 8, 4, 8, 128), F32),
        vmem((4, 3, 64, 128), BF),
        vmem((3, 3, 64, 128), BF),
        vmem((4, 16, 4, 8, 256), F32),
        vmem((4, 4, 128, 256), BF),
        vmem((4, 3, 128, 256), BF),
        vmem((2, 2, 8, 2, 8, 256), F32),
        vmem((4, 2, 2, 64, 128), BF),
        vmem((3, 2, 2, 64, 128), BF),
        vmem((2, 8, 64, 256), F32),
        vmem((2, 8, 64, 256), BF),
        vmem((2, 7, 64, 256), BF),
        vmem((2, 2, 4, 8, 256), F32),
        vmem((2, 4, 16, 256), BF),
        vmem((2, 3, 16, 256), BF),
        vmem((8, 7, 8, 128), F32),
        vmem((7, 7, 8, 128), F32),
        vmem((4, 2, 8, 128), F32),
        vmem((3, 2, 8, 128), F32),
        vmem((3, 3, 8, 128), F32),
        vmem((3, 8, 128), F32),
        vmem((8, 128), F32),
        vmem((15, 8, 128), F32),
        vmem((7, 8, 128), F32),
        dma((4,)), dma((9,)), dma, dma((4,)), dma((4,)), dma((2, 2)), dma((2, 2)),
        dma((2,)), dma, dma((2, 2)), dma((2,)), dma, dma,
        dma((3, 3)), dma((3, 3)), dma((3,)), dma((3,)),
        dma((4, 3)), dma((4, 3)), dma((2, 3)), dma((2, 3)),
        dma((2, 7)), dma((2, 7)), dma((2, 3)), dma((2, 3)),
        dma((2, 7)), dma((2, 7)), dma((3,)), dma((3,)), dma((23,)), dma((23,)),
    ]
    grad_in, grad_kernel = pl.pallas_call(
        body,
        out_shape=(
            jax.ShapeDtypeStruct((2, B, C), BF),
            jax.ShapeDtypeStruct((3, 3, 8, 128), F32),
        ),
        in_specs=[pl.BlockSpec(memory_space=pl.ANY)] * 3,
        out_specs=(pl.BlockSpec(memory_space=pl.ANY), pl.BlockSpec(memory_space=pltpu.VMEM)),
        scratch_shapes=scratch,
        compiler_params=pltpu.CompilerParams(
            collective_id=0, has_side_effects=True, vmem_limit_bytes=52 * 2**20
        ),
        cost_estimate=pl.CostEstimate(flops=14_500_000_000, bytes_accessed=12_000_000, transcendentals=1_600_000),
        name="conv_backward",
    )(pre_act, grad_out, kernel)
    return grad_in, jnp.transpose(grad_kernel, (2, 0, 1, 3))


def solution(mesh):
    in_specs = (P("lat", "lon", None), P("lat", "lon", None), P())
    out_specs = (P("lat", "lon", None), P("lon", None, None, "lat"))
    return jax.shard_map(shards, mesh=mesh, in_specs=in_specs, out_specs=out_specs, check_vma=False)
```

```python
import jax
import jax.numpy as jnp
from jax import lax
from jax.experimental import pallas as pl
from jax.experimental.pallas import tpu as pltpu
from jax.sharding import PartitionSpec as P

BF = jnp.bfloat16
F32 = jnp.float32
MESH = pl.DeviceIdType.MESH
B = 768
C = 512
TN = (((0,), (0,)), ((), ()))
NT = (((1,), (1,)), ((), ()))


def sigmoid(v):
    return 1.0 / (1.0 + jnp.exp(-v))


def body(
    pre_hbm, go_hbm, w_hbm, gin_hbm, gk_ref,
    ext, gos, wv, pre_half, pre_own, act, acc, gin,
    px, send_x, recv_x, mx_own, send_my, recv_my,
    py, send_y, recv_y, my_own, send_mx, recv_mx,
    pz, send_z, recv_z, mz_own, send_mz, recv_mz,
    send_zf, recv_zf, send_xf, recv_xf,
    final, ar_own, ar_core, ar_xy, ar_z,
    ld_sem, w_sem, out_sem, sib_s, sib_r, rim_s, rim_r, halo_s, halo_r, hrim_s, hrim_r, fwd_s, fwd_r,
    x_s, x_r, my_s, my_r, y_s, y_r, mx_s, mx_r, z_s, z_r, mz_s, mz_r, zf_s, zf_r, xf_s, xf_r, ar_s, ar_r,
):
    lat = lax.axis_index("lat")
    lon = lax.axis_index("lon")
    xlo, core = lat // 2, lat % 2
    z, xh, y = lon // 8, (lon // 4) % 2, lon % 4
    x = xh * 2 + xlo

    sib = (xlo * 2 + 1 - core, lon)
    left, right = lax.rem(lon + 63, 64), lax.rem(lon + 1, 64)

    def y_peer(d):
        to = lax.rem(y + d, 4)
        return to, (lat, (z * 2 + xh) * 4 + to)

    def z_peer(d):
        to = lax.rem(z + d, 8)
        return to, (lat, (to * 2 + xh) * 4 + y)

    def x_peer(d):
        to = lax.rem(x + d, 4)
        return to, (lax.rem(to, 2) * 2 + core, (z * 2 + to // 2) * 4 + y)

    def plane_peer(d):
        tx, ty = lax.rem(x + d % 4, 4), lax.rem(y + d // 4, 4)
        return tx * 4 + ty, (lax.rem(tx, 2) * 2 + core, (z * 2 + tx // 2) * 4 + ty)

    def remote(src, dst, ss, rs, dev):
        return pltpu.make_async_remote_copy(
            src_ref=src, dst_ref=dst, send_sem=ss, recv_sem=rs, device_id=dev, device_id_type=MESH
        )

    bar = pltpu.get_barrier_semaphore()
    peers = [z_peer(d)[1] for d in (4, 3, 5, 2, 6, 1, 7)]
    for side in (left, right):
        for q in range(4):
            peers.append((q, side))
    peers += [plane_peer(d)[1] for d in range(1, 16)]
    peers += [((1 - xlo) * 2 + t, lon) for t in range(2)]
    peers.append(sib)
    for p in peers:
        pl.semaphore_signal(bar, inc=1, device_id=p, device_id_type=MESH)

    own = 1 + 2 * core
    loads = [
        pltpu.make_async_copy(go_hbm, ext.at[pl.ds(own, 2), pl.ds(16, B)], ld_sem.at[0]),
        pltpu.make_async_copy(pre_hbm, pre_own, ld_sem.at[1]),
    ]
    for h in range(2):
        loads.append(
            pltpu.make_async_copy(
                pre_hbm.at[:, :, pl.ds(pl.multiple_of(core * 128, 128) + 256 * h, 128)],
                pre_half.at[pl.ds(2 * core, 2), :, pl.ds(128 * h, 128)],
                ld_sem.at[2 + h],
            )
        )
    for cp in loads:
        cp.start()
    pl.semaphore_wait(bar, len(peers))

    sib_copies = []
    for m in range(2):
        sib_copies.append(
            remote(go_hbm.at[m], ext.at[own + m, pl.ds(16, B)], sib_s.at[m], sib_r.at[m], sib)
        )
    for h in range(2):
        sib_copies.append(
            remote(
                pre_hbm.at[:, :, pl.ds(pl.multiple_of((1 - core) * 128, 128) + 256 * h, 128)],
                pre_half.at[pl.ds(2 * core, 2), :, pl.ds(128 * h, 128)],
                sib_s.at[2 + h], sib_r.at[2 + h], sib,
            )
        )
    rims = []
    for t in range(2):
        rims.append(
            remote(
                go_hbm.at[:, pl.ds(B - 16, 16)], ext.at[pl.ds(own, 2), pl.ds(0, 16)],
                rim_s.at[0, t], rim_r.at[0, core], (xlo * 2 + t, right),
            )
        )
        rims.append(
            remote(
                go_hbm.at[:, pl.ds(0, 16)], ext.at[pl.ds(own, 2), pl.ds(16 + B, 16)],
                rim_s.at[1, t], rim_r.at[1, core], (xlo * 2 + t, left),
            )
        )
    for cp in rims:
        cp.start()
    for cp in sib_copies:
        cp.start()

    owner = core + xlo == 1
    far = 5 * xlo
    halos = []
    for t in range(2):
        halos.append(
            remote(
                go_hbm.at[core, pl.ds(384 * t, 384)], ext.at[far, pl.ds(16 + 384 * t, 384)],
                halo_s.at[t], halo_r, ((1 - xlo) * 2 + t, lon),
            )
        )
        halos.append(
            remote(
                go_hbm.at[core, pl.ds(B - 16, 16)], ext.at[far, pl.ds(0, 16)],
                hrim_s.at[0, t], hrim_r.at[0], ((1 - xlo) * 2 + t, right),
            )
        )
        halos.append(
            remote(
                go_hbm.at[core, pl.ds(0, 16)], ext.at[far, pl.ds(16 + B, 16)],
                hrim_s.at[1, t], hrim_r.at[1], ((1 - xlo) * 2 + t, left),
            )
        )

    @pl.when(owner)
    def _():
        for cp in halos:
            cp.start()

    w_loads = []
    for i in range(3):
        for j in range(3):
            cp = pltpu.make_async_copy(w_hbm.at[i, j], wv.at[i, :, pl.ds(512 * j, 512)], w_sem.at[3 * i + j])
            cp.start()
            w_loads.append(cp)

    def centre(r):
        gos[pl.ds(pl.multiple_of(r * B, B), B), 512:1024] = ext[r, 16 : 16 + B, :]

    def sides(r):
        rows = pl.ds(pl.multiple_of(r * B, B), B)
        gos[rows, 0:512] = ext[r, 17 : 17 + B, :]
        gos[rows, 1024:1536] = ext[r, 15 : 15 + B, :]

    def activate(r):
        @pl.loop(0, 3)
        def _(n):
            v = pre_half[r, pl.ds(pl.multiple_of(n * 256, 256), 256), :].astype(F32)
            act[pl.ds(pl.multiple_of(r * B + n * 256, 256), 256), :] = (v * sigmoid(v)).astype(BF)

    zero_row = 5 * xlo
    gos[pl.ds(pl.multiple_of(zero_row * B, B), B), :] = jnp.zeros((B, 1536), BF)

    for cp in loads:
        cp.wait()

    @pl.loop(0, 2)
    def _(m):
        activate(2 * core + m)
        centre(own + m)

    def wait_rims(cc):
        rows = pl.ds(1 + 2 * cc, 2)
        for side, at in ((0, 0), (1, 16 + B)):
            remote(
                ext.at[rows, pl.ds(at, 16)], ext.at[rows, pl.ds(at, 16)],
                rim_s.at[side, 0], rim_r.at[side, cc], sib,
            ).wait_recv()

    def term(j, g0, a0, k):
        return lax.dot_general(
            gos[pl.ds(pl.multiple_of(g0 * B, B), k), pl.ds(pl.multiple_of(j * 512, 512), 512)],
            act[pl.ds(pl.multiple_of(a0 * B, B), k), :],
            TN,
            preferred_element_type=F32,
        )

    def own_rows(j):
        px[j] = term(j, own, 2 * core, 2 * B).reshape(8, 2, 32, 256)

    def own_pair(j):
        return term(j, own + xlo, 2 * core + 1 - xlo, B)

    own_rows(1)
    py[1] = own_pair(1).reshape(16, 4, 8, 256)

    wait_rims(core)

    @pl.loop(0, 2)
    def _(m):
        sides(own + m)

    py[0] = own_pair(0).reshape(16, 4, 8, 256)
    pz[0] = own_pair(2).reshape(8, 64, 256)

    @pl.loop(0, 2)
    def _(n):
        own_rows(2 * n)

    other = 1 + 2 * (1 - core)
    for m in range(2):
        remote(
            ext.at[other + m, pl.ds(16, B)], ext.at[other + m, pl.ds(16, B)], sib_s.at[m], sib_r.at[m], sib
        ).wait_recv()
    for h in range(2):
        part = pre_half.at[pl.ds(2 * (1 - core), 2), :, pl.ds(128 * h, 128)]
        remote(part, part, sib_s.at[2 + h], sib_r.at[2 + h], sib).wait_recv()

    @pl.loop(0, 2)
    def _(m):
        activate(2 * (1 - core) + m)
        centre(other + m)

    def x_copy(j, d):
        to, dev = x_peer(d)
        return remote(send_x.at[j, to], recv_x.at[j, d - 1], x_s.at[j, d - 1], x_r.at[j, d - 1], dev)

    def y_copy(t, d):
        to, dev = y_peer(d)
        return remote(send_y.at[t, to], recv_y.at[t, d - 1], y_s.at[t, d - 1], y_r.at[t, d - 1], dev)

    def z_copy(g, d):
        to, dev = z_peer(d)
        return remote(send_z.at[g, to], recv_z.at[g, d - 1], z_s.at[g, d - 1], z_r.at[g, d - 1], dev)

    def first_x(j):
        p = px[j] + term(j, other, 2 * (1 - core), 2 * B).reshape(8, 2, 32, 256)
        px[j] = p
        for a in range(2):
            for b in range(2):
                send_x[j, 2 * a + b] = p[:, a, :, 128 * b : 128 * b + 128].reshape(256, 128).astype(BF)
        for d in (1, 2, 3):
            x_copy(j, d).start()

    def first_y(t, j, g0, a0, k):
        p = py[t] + term(j, g0, a0, k).reshape(16, 4, 8, 256)
        py[t] = p
        for to in range(4):
            send_y[t, to] = p[:, to].reshape(128, 256).astype(BF)
        for d in (1, 2, 3):
            y_copy(t, d).start()

    def first_z(g, j, g0, a0, k):
        p = pz[g] + term(j, g0, a0, k).reshape(8, 64, 256)
        pz[g] = p
        send_z[g] = p.astype(BF)
        for d in range(1, 8):
            z_copy(g, d).start()

    first_y(1, 1, 2 - core + xlo, 2 - core - xlo, 2 * B)
    wait_rims(1 - core)

    @pl.loop(0, 2)
    def _(m):
        sides(other + m)

    first_y(0, 0, 2 - core + xlo, 2 - core - xlo, 2 * B)
    first_z(0, 2, 2 - core + xlo, 2 - core - xlo, 2 * B)
    first_x(0)

    near = 5 * (1 - xlo)
    half = ext.at[near, pl.ds(pl.multiple_of(16 + 384 * core, 16), 384)]
    other_half = ext.at[near, pl.ds(pl.multiple_of(16 + 384 * (1 - core), 16), 384)]
    remote(half, half, halo_s.at[0], halo_r, sib).wait_recv()
    forward = remote(half, half, fwd_s, fwd_r, sib)
    forward.start()

    first_x(1)

    def local_pairs(j):
        return term(j, 2 - xlo, xlo, 3 * B)

    pz[1] = local_pairs(2).reshape(8, 64, 256)

    @pl.loop(0, 2)
    def _(j):
        py[2 + j] = local_pairs(j).reshape(16, 4, 8, 256)

    for side, at in ((0, 0), (1, 16 + B)):
        edge = ext.at[near, pl.ds(at, 16)]
        remote(edge, edge, hrim_s.at[side, 0], hrim_r.at[side], sib).wait_recv()
    remote(other_half, other_half, fwd_s, fwd_r, sib).wait_recv()
    centre(near)
    sides(near)

    @pl.loop(0, 2)
    def _(j):
        first_y(2 + j, j, near, 3 * (1 - xlo), B)

    first_z(1, 2, near, 3 * (1 - xlo), B)
    first_x(2)

    for cp in w_loads:
        cp.wait()

    def own_share(n):
        m, at = n // 3, lax.rem(n, 3) * 256

        def rows(r):
            return pl.ds(pl.multiple_of(r * B + at, 256), 256)

        here = lax.dot_general(gos[rows(own + m), :], wv[1], NT, preferred_element_type=F32)
        there = lax.dot_general(gos[rows(own + 1 - m), :], wv[2 * m], NT, preferred_element_type=F32)
        acc[pl.ds(pl.multiple_of(n * 256, 256), 256), :] = here + there

    @pl.loop(0, 3)
    def _(n):
        own_share(n)

    def rest(n):
        m, at = n // 3, lax.rem(n, 3) * 256
        src = pl.ds(pl.multiple_of((2 * core + 3 * m) * B + at, 256), 256)
        other_row = lax.dot_general(gos[src, :], wv[2 - 2 * m], NT, preferred_element_type=F32)
        grad = acc[pl.ds(pl.multiple_of(n * 256, 256), 256), :] + other_row
        cells = pl.ds(pl.multiple_of(at, 256), 256)
        h = pre_own[m, cells, :].astype(F32)
        s = sigmoid(h)
        gin[m, cells, :] = (grad * s * (1.0 + h * (1.0 - s))).astype(BF)

    store = pltpu.make_async_copy(gin, gin_hbm, out_sem)

    def my_copy(d):
        to, dev = y_peer(d)
        return remote(send_my.at[to], recv_my.at[d - 1], my_s.at[d - 1], my_r.at[d - 1], dev)

    def mx_copy(gi, d):
        to, dev = x_peer(d)
        return remote(send_mx.at[to, gi], recv_mx.at[d - 1, gi], mx_s.at[gi, d - 1], mx_r.at[gi, d - 1], dev)

    def mz_copy(g, d):
        to, dev = y_peer(d)
        return remote(send_mz.at[g, to], recv_mz.at[g, d - 1], mz_s.at[g, d - 1], mz_r.at[g, d - 1], dev)

    my_lanes = pl.ds(pl.multiple_of(xlo * 128, 128), 128)

    def finish_x():
        @pl.loop(0, 3)
        def _(j):
            total = px[j, :, xh, :, my_lanes].reshape(256, 128)
            for d in (1, 2, 3):
                x_copy(j, d).wait_recv()
                total = total + recv_x[j, d - 1].astype(F32)
            total = total.reshape(8, 4, 8, 128)
            mx_own[j] = total
            for to in range(4):
                send_my[to, j] = total[:, to].reshape(64, 128).astype(BF)

        for d in (1, 2, 3):
            my_copy(d).start()

    def finish_y(g, gi):
        @pl.loop(0, 2)
        def _(j):
            t = 2 * g + j
            total = py[t, :, y].reshape(128, 256)
            for d in (1, 2, 3):
                y_copy(t, d).wait_recv()
                total = total + recv_y[t, d - 1].astype(F32)
            total = total.reshape(8, 2, 8, 256)
            my_own[gi, j] = total
            for a in range(2):
                for b in range(2):
                    part = total[:, a, :, 128 * b : 128 * b + 128]
                    send_mx[2 * a + b, gi, j] = part.reshape(64, 128).astype(BF)

        for d in (1, 2, 3):
            mx_copy(gi, d).start()

    def finish_z(g):
        total = pz[g, z]
        for d in range(1, 8):
            z_copy(g, d).wait_recv()
            total = total + recv_z[g, d - 1].astype(F32)
        total = total.reshape(2, 4, 8, 256)
        mz_own[g] = total
        for to in range(4):
            send_mz[g, to] = total[:, to].reshape(16, 256).astype(BF)
        for d in (1, 2, 3):
            mz_copy(g, d).start()

    finish_x()
    finish_z(0)
    finish_y(0, 1 - xlo)

    @pl.loop(3, 6)
    def _(n):
        own_share(n)

    def zf_copy(part, d):
        to, dev = z_peer(d)
        which = (pl.ds(0, 3), pl.ds(3, 4))[part]
        return remote(
            send_zf.at[to, which], recv_zf.at[d - 1, which], zf_s.at[part, d - 1], zf_r.at[part, d - 1], dev
        )

    def xf_copy(d):
        to, dev = x_peer(d)
        return remote(send_xf.at[to], recv_xf.at[d - 1], xf_s.at[d - 1], xf_r.at[d - 1], dev)

    finish_y(1, xlo)
    finish_z(1)

    for d in (1, 2, 3):
        my_copy(d).wait_recv()

    @pl.loop(0, 3)
    def _(j):
        total = mx_own[j, :, y].reshape(64, 128)
        for d in range(3):
            total = total + recv_my[d, j].astype(F32)
        send_zf[:, j] = total.reshape(8, 8, 128)

    for d in range(1, 8):
        zf_copy(0, d).start()

    @pl.loop(0, 3)
    def _(n):
        rest(n)

    for g in range(2):
        slot = (1 - xlo, xlo)[g]
        total = mz_own[g, :, y].reshape(16, 256)
        for d in (1, 2, 3):
            mz_copy(g, d).wait_recv()
            total = total + recv_mz[g, d - 1].astype(F32)
        for a in range(2):
            for b in range(2):
                send_xf[2 * a + b, slot] = total[8 * a : 8 * a + 8, 128 * b : 128 * b + 128]
    for d in (1, 2, 3):
        xf_copy(d).start()

    for gi in range(2):
        for d in (1, 2, 3):
            mx_copy(gi, d).wait_recv()
        for j in range(2):
            total = my_own[gi, j, :, xh, :, my_lanes].reshape(64, 128)
            for d in range(3):
                total = total + recv_mx[d, gi, j].astype(F32)
            send_zf[:, 3 + 2 * gi + j] = total.reshape(8, 8, 128)
    for d in range(1, 8):
        zf_copy(1, d).start()

    @pl.loop(3, 6)
    def _(n):
        rest(n)

    store.start()

    for d in (1, 2, 3):
        xf_copy(d).wait_recv()
    for gi in range(2):
        final[2 * gi, 2] = send_xf[x, gi] + recv_xf[0, gi] + recv_xf[1, gi] + recv_xf[2, gi]
    for part in range(2):
        total = send_zf[z, pl.ds(3 * part, 3 + part)]
        for d in range(1, 8):
            zf_copy(part, d).wait_recv()
            total = total + recv_zf[d - 1, pl.ds(3 * part, 3 + part)]
        if part == 0:
            final[1] = total
        else:
            for gi in range(2):
                final[2 * gi, 0:2] = total[2 * gi : 2 * gi + 2]

    def drain():
        for cp in rims + sib_copies:
            cp.wait_send()

        @pl.when(owner)
        def _():
            for cp in halos:
                cp.wait_send()

        forward.wait_send()
        for d in (1, 2, 3):
            for j in range(3):
                x_copy(j, d).wait_send()
            for t in range(4):
                y_copy(t, d).wait_send()
            for g in range(2):
                mx_copy(g, d).wait_send()
                mz_copy(g, d).wait_send()
            my_copy(d).wait_send()
            xf_copy(d).wait_send()
        for d in range(1, 8):
            for g in range(2):
                z_copy(g, d).wait_send()
                zf_copy(g, d).wait_send()
        store.wait()

    all_terms = final[...].reshape(9, 8, 128)
    total = jnp.sum(all_terms * all_terms, axis=0)
    ar_own[0] = total
    cp = remote(ar_own.at[0], ar_core, ar_s.at[0], ar_r.at[0], sib)
    cp.start()
    sums = [cp]
    cp.wait_recv()
    total = total + ar_core[...]
    at = 1
    for stage, (peer, count, slots) in enumerate(((plane_peer, 15, ar_xy), (z_peer, 7, ar_z))):
        ar_own[1 + stage] = total
        copies = []
        for d in range(1, count + 1):
            cp = remote(ar_own.at[1 + stage], slots.at[d - 1], ar_s.at[at], ar_r.at[at], peer(d)[1])
            at = at + 1
            cp.start()
            copies.append(cp)
        if stage == 0:
            drain()
        else:
            for cp in sums:
                cp.wait_send()
        for cp in copies:
            cp.wait_recv()
        for d in range(count):
            total = total + slots[d]
        sums = [] if stage else sums
        sums += copies
    grand = jnp.sum(total)
    factor = jnp.float32(3.0 * C) * lax.rsqrt(jnp.full((8, 128), grand, F32) + 1e-06)
    for i in range(3):
        for j in range(3):
            gk_ref[i, j] = final[i, j] * factor

    for cp in sums:
        cp.wait_send()


def shards(pre_act, grad_out, kernel):
    vmem = pltpu.VMEM
    dma = pltpu.SemaphoreType.DMA
    scratch = [
        vmem((6, B + 32, C), BF),
        vmem((6 * B, 3 * C), BF),
        vmem((3, C, 3 * C), BF),
        vmem((4, B, 256), BF),
        vmem((2, B, C), BF),
        vmem((4 * B, 256), BF),
        vmem((2 * B, C), F32),
        vmem((2, B, C), BF),
        vmem((3, 8, 2, 32, 256), F32),
        vmem((3, 4, 256, 128), BF),
        vmem((3, 3, 256, 128), BF),
        vmem((3, 8, 4, 8, 128), F32),
        vmem((4, 3, 64, 128), BF),
        vmem((3, 3, 64, 128), BF),
        vmem((4, 16, 4, 8, 256), F32),
        vmem((4, 4, 128, 256), BF),
        vmem((4, 3, 128, 256), BF),
        vmem((2, 2, 8, 2, 8, 256), F32),
        vmem((4, 2, 2, 64, 128), BF),
        vmem((3, 2, 2, 64, 128), BF),
        vmem((2, 8, 64, 256), F32),
        vmem((2, 8, 64, 256), BF),
        vmem((2, 7, 64, 256), BF),
        vmem((2, 2, 4, 8, 256), F32),
        vmem((2, 4, 16, 256), BF),
        vmem((2, 3, 16, 256), BF),
        vmem((8, 7, 8, 128), F32),
        vmem((7, 7, 8, 128), F32),
        vmem((4, 2, 8, 128), F32),
        vmem((3, 2, 8, 128), F32),
        vmem((3, 3, 8, 128), F32),
        vmem((3, 8, 128), F32),
        vmem((8, 128), F32),
        vmem((15, 8, 128), F32),
        vmem((7, 8, 128), F32),
        dma((4,)), dma((9,)), dma, dma((4,)), dma((4,)), dma((2, 2)), dma((2, 2)),
        dma((2,)), dma, dma((2, 2)), dma((2,)), dma, dma,
        dma((3, 3)), dma((3, 3)), dma((3,)), dma((3,)),
        dma((4, 3)), dma((4, 3)), dma((2, 3)), dma((2, 3)),
        dma((2, 7)), dma((2, 7)), dma((2, 3)), dma((2, 3)),
        dma((2, 7)), dma((2, 7)), dma((3,)), dma((3,)), dma((23,)), dma((23,)),
    ]
    grad_in, grad_kernel = pl.pallas_call(
        body,
        out_shape=(
            jax.ShapeDtypeStruct((2, B, C), BF),
            jax.ShapeDtypeStruct((3, 3, 8, 128), F32),
        ),
        in_specs=[pl.BlockSpec(memory_space=pl.ANY)] * 3,
        out_specs=(pl.BlockSpec(memory_space=pl.ANY), pl.BlockSpec(memory_space=pltpu.VMEM)),
        scratch_shapes=scratch,
        compiler_params=pltpu.CompilerParams(
            collective_id=0, has_side_effects=True, vmem_limit_bytes=52 * 2**20
        ),
        cost_estimate=pl.CostEstimate(flops=14_500_000_000, bytes_accessed=12_000_000, transcendentals=1_600_000),
        name="conv_backward",
    )(pre_act, grad_out, kernel)
    return grad_in, jnp.transpose(grad_kernel, (2, 0, 1, 3))


def solution(mesh):
    in_specs = (P("lat", "lon", None), P("lat", "lon", None), P())
    out_specs = (P("lat", "lon", None), P("lon", None, None, "lat"))
    return jax.shard_map(shards, mesh=mesh, in_specs=in_specs, out_specs=out_specs, check_vma=False)
```

```python
import jax
import jax.numpy as jnp
from jax import lax
from jax.experimental import pallas as pl
from jax.experimental.pallas import tpu as pltpu
from jax.sharding import PartitionSpec as P

BF = jnp.bfloat16
F32 = jnp.float32
MESH = pl.DeviceIdType.MESH
B = 768
C = 512
TN = (((0,), (0,)), ((), ()))
NT = (((1,), (1,)), ((), ()))
FAR_Z = (4, 3, 5, 2, 6, 1, 7)
FAR_XY = (10, 6, 14, 9, 11, 5, 7, 13, 15, 2, 8, 1, 3, 4, 12)


def sigmoid(v):
    return 1.0 / (1.0 + jnp.exp(-v))


def body(
    pre_hbm, go_hbm, w_hbm, gin_hbm, gk_ref,
    ext, gos, wv, pre_half, pre_own, act, acc, gin,
    px, send_x, recv_x, mx_own, send_my, recv_my,
    py, send_y, recv_y, my_own, send_mx, recv_mx,
    pz, send_z, recv_z, mz_own, send_mz, recv_mz,
    send_zf, recv_zf, send_xf, recv_xf,
    final, ar_own, ar_core, ar_xy, ar_z,
    ld_sem, w_sem, out_sem, sib_s, sib_r, rim_s, rim_r, halo_s, halo_r, hrim_s, hrim_r, fwd_s, fwd_r,
    x_s, x_r, my_s, my_r, y_s, y_r, mx_s, mx_r, z_s, z_r, mz_s, mz_r, zf_s, zf_r, xf_s, xf_r, ar_s, ar_r,
):
    lat = lax.axis_index("lat")
    lon = lax.axis_index("lon")
    xlo, core = lat // 2, lat % 2
    z, xh, y = lon // 8, (lon // 4) % 2, lon % 4
    x = xh * 2 + xlo

    sib = (xlo * 2 + 1 - core, lon)
    left, right = lax.rem(lon + 63, 64), lax.rem(lon + 1, 64)

    def y_peer(d):
        to = lax.rem(y + d, 4)
        return to, (lat, (z * 2 + xh) * 4 + to)

    def z_peer(d):
        to = lax.rem(z + d, 8)
        return to, (lat, (to * 2 + xh) * 4 + y)

    def x_peer(d):
        to = lax.rem(x + d, 4)
        return to, (lax.rem(to, 2) * 2 + core, (z * 2 + to // 2) * 4 + y)

    def plane_peer(d):
        tx, ty = lax.rem(x + d % 4, 4), lax.rem(y + d // 4, 4)
        return tx * 4 + ty, (lax.rem(tx, 2) * 2 + core, (z * 2 + tx // 2) * 4 + ty)

    def remote(src, dst, ss, rs, dev):
        return pltpu.make_async_remote_copy(
            src_ref=src, dst_ref=dst, send_sem=ss, recv_sem=rs, device_id=dev, device_id_type=MESH
        )

    bar = pltpu.get_barrier_semaphore()
    peers = [z_peer(d)[1] for d in (4, 3, 5, 2, 6, 1, 7)]
    for side in (left, right):
        for q in range(4):
            peers.append((q, side))
    peers += [plane_peer(d)[1] for d in range(1, 16)]
    peers += [((1 - xlo) * 2 + t, lon) for t in range(2)]
    peers.append(sib)
    for p in peers:
        pl.semaphore_signal(bar, inc=1, device_id=p, device_id_type=MESH)

    own = 1 + 2 * core
    loads = [
        pltpu.make_async_copy(go_hbm, ext.at[pl.ds(own, 2), pl.ds(16, B)], ld_sem.at[0]),
        pltpu.make_async_copy(pre_hbm, pre_own, ld_sem.at[1]),
    ]
    for h in range(2):
        loads.append(
            pltpu.make_async_copy(
                pre_hbm.at[:, :, pl.ds(pl.multiple_of(core * 128, 128) + 256 * h, 128)],
                pre_half.at[pl.ds(2 * core, 2), :, pl.ds(128 * h, 128)],
                ld_sem.at[2 + h],
            )
        )
    for cp in loads:
        cp.start()
    pl.semaphore_wait(bar, len(peers))

    sib_copies = []
    for m in range(2):
        sib_copies.append(
            remote(go_hbm.at[m], ext.at[own + m, pl.ds(16, B)], sib_s.at[m], sib_r.at[m], sib)
        )
    for h in range(2):
        sib_copies.append(
            remote(
                pre_hbm.at[:, :, pl.ds(pl.multiple_of((1 - core) * 128, 128) + 256 * h, 128)],
                pre_half.at[pl.ds(2 * core, 2), :, pl.ds(128 * h, 128)],
                sib_s.at[2 + h], sib_r.at[2 + h], sib,
            )
        )
    rims = []
    for t in range(2):
        rims.append(
            remote(
                go_hbm.at[:, pl.ds(B - 16, 16)], ext.at[pl.ds(own, 2), pl.ds(0, 16)],
                rim_s.at[0, t], rim_r.at[0, core], (xlo * 2 + t, right),
            )
        )
        rims.append(
            remote(
                go_hbm.at[:, pl.ds(0, 16)], ext.at[pl.ds(own, 2), pl.ds(16 + B, 16)],
                rim_s.at[1, t], rim_r.at[1, core], (xlo * 2 + t, left),
            )
        )
    for cp in rims:
        cp.start()
    for cp in sib_copies:
        cp.start()

    owner = core + xlo == 1
    far = 5 * xlo
    halos = []
    for t in range(2):
        halos.append(
            remote(
                go_hbm.at[core, pl.ds(384 * t, 384)], ext.at[far, pl.ds(16 + 384 * t, 384)],
                halo_s.at[t], halo_r, ((1 - xlo) * 2 + t, lon),
            )
        )
        halos.append(
            remote(
                go_hbm.at[core, pl.ds(B - 16, 16)], ext.at[far, pl.ds(0, 16)],
                hrim_s.at[0, t], hrim_r.at[0], ((1 - xlo) * 2 + t, right),
            )
        )
        halos.append(
            remote(
                go_hbm.at[core, pl.ds(0, 16)], ext.at[far, pl.ds(16 + B, 16)],
                hrim_s.at[1, t], hrim_r.at[1], ((1 - xlo) * 2 + t, left),
            )
        )

    @pl.when(owner)
    def _():
        for cp in halos:
            cp.start()

    w_loads = []
    for i in range(3):
        for j in range(3):
            cp = pltpu.make_async_copy(w_hbm.at[i, j], wv.at[i, :, pl.ds(512 * j, 512)], w_sem.at[3 * i + j])
            cp.start()
            w_loads.append(cp)

    def centre(r):
        gos[pl.ds(pl.multiple_of(r * B, B), B), 512:1024] = ext[r, 16 : 16 + B, :]

    def sides(r):
        rows = pl.ds(pl.multiple_of(r * B, B), B)
        gos[rows, 0:512] = ext[r, 17 : 17 + B, :]
        gos[rows, 1024:1536] = ext[r, 15 : 15 + B, :]

    def activate(r):
        @pl.loop(0, 3)
        def _(n):
            v = pre_half[r, pl.ds(pl.multiple_of(n * 256, 256), 256), :].astype(F32)
            act[pl.ds(pl.multiple_of(r * B + n * 256, 256), 256), :] = (v * sigmoid(v)).astype(BF)

    zero_row = 5 * xlo
    gos[pl.ds(pl.multiple_of(zero_row * B, B), B), :] = jnp.zeros((B, 1536), BF)

    for cp in loads:
        cp.wait()

    @pl.loop(0, 2)
    def _(m):
        activate(2 * core + m)
        centre(own + m)

    def wait_rims(cc):
        rows = pl.ds(1 + 2 * cc, 2)
        for side, at in ((0, 0), (1, 16 + B)):
            remote(
                ext.at[rows, pl.ds(at, 16)], ext.at[rows, pl.ds(at, 16)],
                rim_s.at[side, 0], rim_r.at[side, cc], sib,
            ).wait_recv()

    def term(j, g0, a0, k):
        return lax.dot_general(
            gos[pl.ds(pl.multiple_of(g0 * B, B), k), pl.ds(pl.multiple_of(j * 512, 512), 512)],
            act[pl.ds(pl.multiple_of(a0 * B, B), k), :],
            TN,
            preferred_element_type=F32,
        )

    def own_rows(j):
        px[j] = term(j, own, 2 * core, 2 * B).reshape(8, 2, 32, 256)

    def own_pair(j):
        return term(j, own + xlo, 2 * core + 1 - xlo, B)

    own_rows(1)
    py[1] = own_pair(1).reshape(16, 4, 8, 256)

    wait_rims(core)

    @pl.loop(0, 2)
    def _(m):
        sides(own + m)

    py[0] = own_pair(0).reshape(16, 4, 8, 256)
    pz[0] = own_pair(2).reshape(8, 64, 256)

    @pl.loop(0, 2)
    def _(n):
        own_rows(2 * n)

    other = 1 + 2 * (1 - core)
    for m in range(2):
        remote(
            ext.at[other + m, pl.ds(16, B)], ext.at[other + m, pl.ds(16, B)], sib_s.at[m], sib_r.at[m], sib
        ).wait_recv()
    for h in range(2):
        part = pre_half.at[pl.ds(2 * (1 - core), 2), :, pl.ds(128 * h, 128)]
        remote(part, part, sib_s.at[2 + h], sib_r.at[2 + h], sib).wait_recv()

    @pl.loop(0, 2)
    def _(m):
        activate(2 * (1 - core) + m)
        centre(other + m)

    def x_copy(j, d):
        to, dev = x_peer(d)
        return remote(send_x.at[j, to], recv_x.at[j, d - 1], x_s.at[j, d - 1], x_r.at[j, d - 1], dev)

    def y_copy(t, d):
        to, dev = y_peer(d)
        return remote(send_y.at[t, to], recv_y.at[t, d - 1], y_s.at[t, d - 1], y_r.at[t, d - 1], dev)

    def z_copy(g, d):
        to, dev = z_peer(d)
        return remote(send_z.at[g, to], recv_z.at[g, d - 1], z_s.at[g, d - 1], z_r.at[g, d - 1], dev)

    def first_x(j):
        p = px[j] + term(j, other, 2 * (1 - core), 2 * B).reshape(8, 2, 32, 256)
        px[j] = p
        for a in range(2):
            for b in range(2):
                send_x[j, 2 * a + b] = p[:, a, :, 128 * b : 128 * b + 128].reshape(256, 128).astype(BF)
        for d in (1, 2, 3):
            x_copy(j, d).start()

    def first_y(t, j, g0, a0, k):
        p = py[t] + term(j, g0, a0, k).reshape(16, 4, 8, 256)
        py[t] = p
        for to in range(4):
            send_y[t, to] = p[:, to].reshape(128, 256).astype(BF)
        for d in (1, 2, 3):
            y_copy(t, d).start()

    def first_z(g, j, g0, a0, k):
        p = pz[g] + term(j, g0, a0, k).reshape(8, 64, 256)
        pz[g] = p
        send_z[g] = p.astype(BF)
        for d in range(1, 8):
            z_copy(g, d).start()

    first_y(1, 1, 2 - core + xlo, 2 - core - xlo, 2 * B)
    wait_rims(1 - core)

    @pl.loop(0, 2)
    def _(m):
        sides(other + m)

    first_y(0, 0, 2 - core + xlo, 2 - core - xlo, 2 * B)
    first_z(0, 2, 2 - core + xlo, 2 - core - xlo, 2 * B)
    first_x(0)

    near = 5 * (1 - xlo)
    half = ext.at[near, pl.ds(pl.multiple_of(16 + 384 * core, 16), 384)]
    other_half = ext.at[near, pl.ds(pl.multiple_of(16 + 384 * (1 - core), 16), 384)]
    remote(half, half, halo_s.at[0], halo_r, sib).wait_recv()
    forward = remote(half, half, fwd_s, fwd_r, sib)
    forward.start()

    first_x(1)

    def local_pairs(j):
        return term(j, 2 - xlo, xlo, 3 * B)

    pz[1] = local_pairs(2).reshape(8, 64, 256)

    @pl.loop(0, 2)
    def _(j):
        py[2 + j] = local_pairs(j).reshape(16, 4, 8, 256)

    for side, at in ((0, 0), (1, 16 + B)):
        edge = ext.at[near, pl.ds(at, 16)]
        remote(edge, edge, hrim_s.at[side, 0], hrim_r.at[side], sib).wait_recv()
    remote(other_half, other_half, fwd_s, fwd_r, sib).wait_recv()
    centre(near)
    sides(near)

    @pl.loop(0, 2)
    def _(j):
        first_y(2 + j, j, near, 3 * (1 - xlo), B)

    first_z(1, 2, near, 3 * (1 - xlo), B)
    first_x(2)

    for cp in w_loads:
        cp.wait()

    def own_share(n):
        m, at = n // 3, lax.rem(n, 3) * 256

        def rows(r):
            return pl.ds(pl.multiple_of(r * B + at, 256), 256)

        here = lax.dot_general(gos[rows(own + m), :], wv[1], NT, preferred_element_type=F32)
        there = lax.dot_general(gos[rows(own + 1 - m), :], wv[2 * m], NT, preferred_element_type=F32)
        acc[pl.ds(pl.multiple_of(n * 256, 256), 256), :] = here + there

    @pl.loop(0, 3)
    def _(n):
        own_share(n)

    def rest(n):
        m, at = n // 3, lax.rem(n, 3) * 256
        src = pl.ds(pl.multiple_of((2 * core + 3 * m) * B + at, 256), 256)
        other_row = lax.dot_general(gos[src, :], wv[2 - 2 * m], NT, preferred_element_type=F32)
        grad = acc[pl.ds(pl.multiple_of(n * 256, 256), 256), :] + other_row
        cells = pl.ds(pl.multiple_of(at, 256), 256)
        h = pre_own[m, cells, :].astype(F32)
        s = sigmoid(h)
        gin[m, cells, :] = (grad * s * (1.0 + h * (1.0 - s))).astype(BF)

    store = pltpu.make_async_copy(gin, gin_hbm, out_sem)

    def my_copy(d):
        to, dev = y_peer(d)
        return remote(send_my.at[to], recv_my.at[d - 1], my_s.at[d - 1], my_r.at[d - 1], dev)

    def mx_copy(gi, d):
        to, dev = x_peer(d)
        return remote(send_mx.at[to, gi], recv_mx.at[d - 1, gi], mx_s.at[gi, d - 1], mx_r.at[gi, d - 1], dev)

    def mz_copy(g, d):
        to, dev = y_peer(d)
        return remote(send_mz.at[g, to], recv_mz.at[g, d - 1], mz_s.at[g, d - 1], mz_r.at[g, d - 1], dev)

    my_lanes = pl.ds(pl.multiple_of(xlo * 128, 128), 128)

    def finish_x():
        @pl.loop(0, 3)
        def _(j):
            total = px[j, :, xh, :, my_lanes].reshape(256, 128)
            for d in (1, 2, 3):
                x_copy(j, d).wait_recv()
                total = total + recv_x[j, d - 1].astype(F32)
            total = total.reshape(8, 4, 8, 128)
            mx_own[j] = total
            for to in range(4):
                send_my[to, j] = total[:, to].reshape(64, 128).astype(BF)

        for d in (1, 2, 3):
            my_copy(d).start()

    def finish_y(g, gi):
        @pl.loop(0, 2)
        def _(j):
            t = 2 * g + j
            total = py[t, :, y].reshape(128, 256)
            for d in (1, 2, 3):
                y_copy(t, d).wait_recv()
                total = total + recv_y[t, d - 1].astype(F32)
            total = total.reshape(8, 2, 8, 256)
            my_own[gi, j] = total
            for a in range(2):
                for b in range(2):
                    part = total[:, a, :, 128 * b : 128 * b + 128]
                    send_mx[2 * a + b, gi, j] = part.reshape(64, 128).astype(BF)

        for d in (1, 2, 3):
            mx_copy(gi, d).start()

    def finish_z(g):
        total = pz[g, z]
        for d in range(1, 8):
            z_copy(g, d).wait_recv()
            total = total + recv_z[g, d - 1].astype(F32)
        total = total.reshape(2, 4, 8, 256)
        mz_own[g] = total
        for to in range(4):
            send_mz[g, to] = total[:, to].reshape(16, 256).astype(BF)
        for d in (1, 2, 3):
            mz_copy(g, d).start()

    finish_x()
    finish_z(0)
    finish_y(0, 1 - xlo)

    @pl.loop(3, 6)
    def _(n):
        own_share(n)

    def zf_copy(part, d):
        to, dev = z_peer(d)
        which = (pl.ds(0, 3), pl.ds(3, 4))[part]
        return remote(
            send_zf.at[to, which], recv_zf.at[d - 1, which], zf_s.at[part, d - 1], zf_r.at[part, d - 1], dev
        )

    def xf_copy(d):
        to, dev = x_peer(d)
        return remote(send_xf.at[to], recv_xf.at[d - 1], xf_s.at[d - 1], xf_r.at[d - 1], dev)

    finish_y(1, xlo)
    finish_z(1)

    for d in (1, 2, 3):
        my_copy(d).wait_recv()

    @pl.loop(0, 3)
    def _(j):
        total = mx_own[j, :, y].reshape(64, 128)
        for d in range(3):
            total = total + recv_my[d, j].astype(F32)
        send_zf[:, j] = total.reshape(8, 8, 128)

    for d in range(1, 8):
        zf_copy(0, d).start()

    @pl.loop(0, 3)
    def _(n):
        rest(n)

    for g in range(2):
        slot = (1 - xlo, xlo)[g]
        total = mz_own[g, :, y].reshape(16, 256)
        for d in (1, 2, 3):
            mz_copy(g, d).wait_recv()
            total = total + recv_mz[g, d - 1].astype(F32)
        for a in range(2):
            for b in range(2):
                send_xf[2 * a + b, slot] = total[8 * a : 8 * a + 8, 128 * b : 128 * b + 128]
    for d in (1, 2, 3):
        xf_copy(d).start()

    for gi in range(2):
        for d in (1, 2, 3):
            mx_copy(gi, d).wait_recv()
        for j in range(2):
            total = my_own[gi, j, :, xh, :, my_lanes].reshape(64, 128)
            for d in range(3):
                total = total + recv_mx[d, gi, j].astype(F32)
            send_zf[:, 3 + 2 * gi + j] = total.reshape(8, 8, 128)
    for d in FAR_Z:
        zf_copy(1, d).start()

    @pl.loop(3, 6)
    def _(n):
        rest(n)

    store.start()

    for d in (1, 2, 3):
        xf_copy(d).wait_recv()
    for gi in range(2):
        final[2 * gi, 2] = send_xf[x, gi] + recv_xf[0, gi] + recv_xf[1, gi] + recv_xf[2, gi]
    for part in range(2):
        total = send_zf[z, pl.ds(3 * part, 3 + part)]
        for d in range(1, 8):
            zf_copy(part, d).wait_recv()
            total = total + recv_zf[d - 1, pl.ds(3 * part, 3 + part)]
        if part == 0:
            final[1] = total
        else:
            for gi in range(2):
                final[2 * gi, 0:2] = total[2 * gi : 2 * gi + 2]

    def drain():
        for cp in rims + sib_copies:
            cp.wait_send()

        @pl.when(owner)
        def _():
            for cp in halos:
                cp.wait_send()

        forward.wait_send()
        for d in (1, 2, 3):
            for j in range(3):
                x_copy(j, d).wait_send()
            for t in range(4):
                y_copy(t, d).wait_send()
            for g in range(2):
                mx_copy(g, d).wait_send()
                mz_copy(g, d).wait_send()
            my_copy(d).wait_send()
            xf_copy(d).wait_send()
        for d in range(1, 8):
            for g in range(2):
                z_copy(g, d).wait_send()
                zf_copy(g, d).wait_send()
        store.wait()

    all_terms = final[...].reshape(9, 8, 128)
    total = jnp.sum(all_terms * all_terms, axis=0)
    ar_own[0] = total
    cp = remote(ar_own.at[0], ar_core, ar_s.at[0], ar_r.at[0], sib)
    cp.start()
    sums = [cp]
    cp.wait_recv()
    total = total + ar_core[...]
    at = 1
    for stage, (peer, order, slots) in enumerate(((plane_peer, FAR_XY, ar_xy), (z_peer, FAR_Z, ar_z))):
        ar_own[1 + stage] = total
        copies = []
        for d in order:
            cp = remote(ar_own.at[1 + stage], slots.at[d - 1], ar_s.at[at], ar_r.at[at], peer(d)[1])
            at = at + 1
            cp.start()
            copies.append(cp)
        if stage == 0:
            drain()
        else:
            for cp in sums:
                cp.wait_send()
        for cp in copies:
            cp.wait_recv()
        for d in range(len(order)):
            total = total + slots[d]
        sums = [] if stage else sums
        sums += copies
    grand = jnp.sum(total)
    factor = jnp.float32(3.0 * C) * lax.rsqrt(jnp.full((8, 128), grand, F32) + 1e-06)
    for i in range(3):
        for j in range(3):
            gk_ref[i, j] = final[i, j] * factor

    for cp in sums:
        cp.wait_send()


def shards(pre_act, grad_out, kernel):
    vmem = pltpu.VMEM
    dma = pltpu.SemaphoreType.DMA
    scratch = [
        vmem((6, B + 32, C), BF),
        vmem((6 * B, 3 * C), BF),
        vmem((3, C, 3 * C), BF),
        vmem((4, B, 256), BF),
        vmem((2, B, C), BF),
        vmem((4 * B, 256), BF),
        vmem((2 * B, C), F32),
        vmem((2, B, C), BF),
        vmem((3, 8, 2, 32, 256), F32),
        vmem((3, 4, 256, 128), BF),
        vmem((3, 3, 256, 128), BF),
        vmem((3, 8, 4, 8, 128), F32),
        vmem((4, 3, 64, 128), BF),
        vmem((3, 3, 64, 128), BF),
        vmem((4, 16, 4, 8, 256), F32),
        vmem((4, 4, 128, 256), BF),
        vmem((4, 3, 128, 256), BF),
        vmem((2, 2, 8, 2, 8, 256), F32),
        vmem((4, 2, 2, 64, 128), BF),
        vmem((3, 2, 2, 64, 128), BF),
        vmem((2, 8, 64, 256), F32),
        vmem((2, 8, 64, 256), BF),
        vmem((2, 7, 64, 256), BF),
        vmem((2, 2, 4, 8, 256), F32),
        vmem((2, 4, 16, 256), BF),
        vmem((2, 3, 16, 256), BF),
        vmem((8, 7, 8, 128), F32),
        vmem((7, 7, 8, 128), F32),
        vmem((4, 2, 8, 128), F32),
        vmem((3, 2, 8, 128), F32),
        vmem((3, 3, 8, 128), F32),
        vmem((3, 8, 128), F32),
        vmem((8, 128), F32),
        vmem((15, 8, 128), F32),
        vmem((7, 8, 128), F32),
        dma((4,)), dma((9,)), dma, dma((4,)), dma((4,)), dma((2, 2)), dma((2, 2)),
        dma((2,)), dma, dma((2, 2)), dma((2,)), dma, dma,
        dma((3, 3)), dma((3, 3)), dma((3,)), dma((3,)),
        dma((4, 3)), dma((4, 3)), dma((2, 3)), dma((2, 3)),
        dma((2, 7)), dma((2, 7)), dma((2, 3)), dma((2, 3)),
        dma((2, 7)), dma((2, 7)), dma((3,)), dma((3,)), dma((23,)), dma((23,)),
    ]
    grad_in, grad_kernel = pl.pallas_call(
        body,
        out_shape=(
            jax.ShapeDtypeStruct((2, B, C), BF),
            jax.ShapeDtypeStruct((3, 3, 8, 128), F32),
        ),
        in_specs=[pl.BlockSpec(memory_space=pl.ANY)] * 3,
        out_specs=(pl.BlockSpec(memory_space=pl.ANY), pl.BlockSpec(memory_space=pltpu.VMEM)),
        scratch_shapes=scratch,
        compiler_params=pltpu.CompilerParams(
            collective_id=0, has_side_effects=True, vmem_limit_bytes=52 * 2**20
        ),
        cost_estimate=pl.CostEstimate(flops=14_500_000_000, bytes_accessed=12_000_000, transcendentals=1_600_000),
        name="conv_backward",
    )(pre_act, grad_out, kernel)
    return grad_in, jnp.transpose(grad_kernel, (2, 0, 1, 3))


def solution(mesh):
    in_specs = (P("lat", "lon", None), P("lat", "lon", None), P())
    out_specs = (P("lat", "lon", None), P("lon", None, None, "lat"))
    return jax.shard_map(shards, mesh=mesh, in_specs=in_specs, out_specs=out_specs, check_vma=False)
```
